32 devices in a mesh: rows: 8 (over z, y), cols: 4 (over x, core).
Axes of the slice: x: 2, y: 2, z: 4, core: 2. Of those that a mesh axis runs over, the one named last changes fastest.
Arguments:
- sources: bfloat16 [262144, 128], P(('rows', 'cols')), may hold values from -6 to 6
- tiles: bfloat16 [16384, 128, 128], P(('rows', 'cols')), may hold values from -0.1875 to 0.1875
- block_list: int32 [16384, 2], P(('rows', 'cols')), may hold values from 0 to 2047, as said below
- inverses: bfloat16 [2048, 128, 128], P(('rows', 'cols')), may hold values from -0.5 to 0.5
- slot_cluster: int32 [2048], replicated, may hold values from 0 to 2047, as said below
Outputs:
- near: bfloat16 [262144, 128], P(('rows', 'cols'))
- preconditioned: bfloat16 [262144, 128], P(('rows', 'cols'))
The draws below stay inside these ranges and needn't reach their ends.
Inputs may be any that keep to these rules, and one draw needn't show every extreme that they name: `block_list`: the blocks held on rows index r have row clusters among r*256 to (r+1)*256 - 1; each such cluster is the row of exactly 8 of that group's blocks, one of them its diagonal block; every column cluster lies within 128 clusters of its row cluster. For each device of its group, each device holds exactly 128 blocks whose row cluster that device owns, where device d owns clusters d*64 to (d+1)*64 - 1. `slot_cluster`: A permutation of the clusters. Device d owns clusters d*64 to (d+1)*64 - 1 and the slots with the same numbers; no device's slots hold more than 2 of one device's clusters, and this bound is reached.
All inputs are finite; a program needn't handle non-finite values.
Results may differ from the reference program's by a relative error of at most 0.005.
Values may be sent and summed in bfloat16 or wider, within the bound.
No kernel may reach another device: no remote copies, remote signals or barrier semaphores. Data moves between devices by JAX's collectives and lax.ppermute only.
A program may use at most 192 MiB of HBM per device.

```python
import math
import jax
import jax.numpy as jnp
from jax import lax

B = 128
R = 128
CLUSTERS_DEVICE = 64
NEAR_PER_ROW = 8
OWNERS = 32
GROUP_ROW_SPAN = 256
HW = 128
CLUSTER_TOTAL = 2048
NTILES = 16384
NUNK = 262144


def permute_group(key, length):
    return jax.random.permutation(key, length).astype(jnp.int32)


def draw_block_list(key, part):
    device_groups = CLUSTER_TOTAL // GROUP_ROW_SPAN
    count_per_group = GROUP_ROW_SPAN * NEAR_PER_ROW
    group_members = GROUP_ROW_SPAN // CLUSTERS_DEVICE
    per_owner = CLUSTERS_DEVICE * NEAR_PER_ROW
    piece = per_owner // group_members
    first_key, second_key = jax.random.split(key)
    shuffle_key, device_key = jax.random.split(second_key)
    local_part = jnp.repeat(jnp.arange(GROUP_ROW_SPAN, dtype=jnp.int32), NEAR_PER_ROW)
    every_row = jnp.arange(device_groups, dtype=jnp.int32)[:, None] * GROUP_ROW_SPAN + local_part[None, :]
    offsets = jax.random.randint(first_key, (device_groups, count_per_group), -HW, HW + 1, dtype=jnp.int32)
    position = jnp.arange(count_per_group, dtype=jnp.int32)[None, :]
    offsets = jnp.where(position % NEAR_PER_ROW == 0, 0, offsets)
    offsets = jnp.where(position == 1, HW, jnp.where(position == 2, -HW, offsets))
    column_all = jnp.clip(every_row + offsets, 0, CLUSTER_TOTAL - 1)
    owner_keys = jax.random.split(shuffle_key, device_groups * group_members)
    owner_orders = jax.vmap(lambda one: permute_group(one, per_owner))(owner_keys).reshape(device_groups, group_members, per_owner)
    rows_owner = jnp.take_along_axis(every_row.reshape(device_groups, group_members, per_owner), owner_orders, axis=2)
    column_owner = jnp.take_along_axis(column_all.reshape(device_groups, group_members, per_owner), owner_orders, axis=2)
    rows_dev = rows_owner.reshape(device_groups, group_members, group_members, piece).transpose(0, 2, 1, 3).reshape(device_groups * group_members, per_owner)
    column_dev = column_owner.reshape(device_groups, group_members, group_members, piece).transpose(0, 2, 1, 3).reshape(device_groups * group_members, per_owner)
    device_keys = jax.random.split(device_key, device_groups * group_members)
    device_orders = jax.vmap(lambda one: permute_group(one, per_owner))(device_keys)
    rows_dev = jnp.take_along_axis(rows_dev, device_orders, axis=1)
    column_dev = jnp.take_along_axis(column_dev, device_orders, axis=1)
    return jnp.stack([rows_dev, column_dev], -1).reshape(NTILES, 2).astype(jnp.int32)


def draw_slot_cluster(key, part):
    first_key, second_key = jax.random.split(key)
    score_key, head_key = jax.random.split(jax.random.fold_in(first_key, 7))
    values = jnp.arange(OWNERS, dtype=jnp.int32)
    scores = permute_group(score_key, OWNERS)
    scores = jnp.where(values == 1, -3, jnp.where(values == OWNERS - 1, -2, jnp.where(values == OWNERS // 2, -1, scores)))
    shifts = jnp.argsort(scores, stable=True).astype(jnp.int32)
    leading = min(CLUSTERS_DEVICE, OWNERS)
    head_order = permute_group(head_key, leading)
    shifts = jnp.concatenate([shifts[:leading][head_order], shifts[leading:]], 0).astype(jnp.int32)
    keys = jax.random.split(second_key, OWNERS)
    orders = jax.vmap(lambda one: permute_group(one, CLUSTERS_DEVICE))(keys)
    device = jnp.arange(OWNERS, dtype=jnp.int32)[:, None]
    within = jnp.arange(CLUSTERS_DEVICE, dtype=jnp.int32)[None, :]
    anchor = (device - shifts[within % OWNERS]) % OWNERS
    chosen = orders[anchor, jnp.broadcast_to(within, anchor.shape)]
    return (anchor * CLUSTERS_DEVICE + chosen).reshape(CLUSTER_TOTAL).astype(jnp.int32)


def shard_levels(rng, extent, cuts, smallest, top_value):
    level = 1.0
    for axis_at, parts in cuts:
        heights = jax.random.uniform(jax.random.fold_in(jax.random.fold_in(rng, 6), axis_at), (parts,), jnp.float32, smallest / len(cuts), top_value / len(cuts))
        level = level * jnp.repeat(jnp.exp(heights), extent[axis_at] // parts).reshape((-1,) + (1,) * (len(extent) - 1 - axis_at))
    return level


def normal_values(key, dims, spread, limit, cuts=(), kind=jnp.bfloat16):
    array = spread * jax.random.normal(key, dims, jnp.float32)
    if cuts:
        array = array * shard_levels(key, dims, cuts, -0.22, 0.18)
    return jnp.clip(array, -limit, limit).astype(kind)


def setup_inputs(seed: int = 0) -> dict:
    streams_of = jax.random.split(jax.random.key(seed), 6)
    return {
        "sources": normal_values(streams_of[0], (NUNK, R), 1.0, 6.0, ((0, 32),)),
        "tiles": normal_values(streams_of[1], (NTILES, B, B), (B * NEAR_PER_ROW) ** -0.5, 0.1875, ((0, 32),)),
        "block_list": draw_block_list(jax.random.fold_in(streams_of[5], 71), 0),
        "inverses": normal_values(streams_of[3], (CLUSTER_TOTAL, B, B), B ** -0.5, 0.5, ((0, 32),)),
        "slot_cluster": draw_slot_cluster(jax.random.fold_in(streams_of[5], 71), 0),
    }


def reference(sources, tiles, block_list, inverses, slot_cluster):
    cluster_size = tiles.shape[1]
    columns = sources.shape[1]
    count = sources.shape[0] // cluster_size
    source_blocks = sources.reshape(count, cluster_size, columns)
    step = math.gcd(tiles.shape[0], 1024)

    def add_block(totals, pieces):
        tile_block, pairs = pieces
        picked = source_blocks[pairs[:, 1]].astype(jnp.float32)
        product = jnp.einsum("tij,tjr->tir", tile_block.astype(jnp.float32), picked)
        return totals.at[pairs[:, 0]].add(product), None

    start = jnp.zeros((count, cluster_size, columns), jnp.float32)
    totals, unused = lax.scan(add_block, start, (tiles.reshape(-1, step, cluster_size, cluster_size), block_list.reshape(-1, step, 2)))
    near_blocks = totals.astype(jnp.bfloat16)
    picked = near_blocks[slot_cluster].astype(jnp.float32)
    applied = jnp.einsum("sij,sjr->sir", inverses.astype(jnp.float32), picked).astype(jnp.bfloat16)
    result = jnp.zeros_like(near_blocks).at[slot_cluster].set(applied)
    return near_blocks.reshape(count * cluster_size, columns), result.reshape(count * cluster_size, columns)
```

```python
import functools

import jax
import jax.numpy as jnp
from jax import lax
from jax.experimental import pallas as pl
from jax.experimental.pallas import tpu as pltpu
from jax.sharding import PartitionSpec as P

AXES = ("rows", "cols")
MIB = 1024 * 1024
ANY = pl.BlockSpec(memory_space=pl.ANY)
SMEM = pl.BlockSpec(memory_space=pltpu.SMEM)


def pack_kernel(meta_ref, bucket_ref, tiles, keep, send, meta_keep, meta_send, counts, sem):
    total = tiles.shape[0]
    half = total // 2
    quarter = total // 4
    for first in (0, 3):
        counts[first] = 0
        counts[first + 1] = quarter
        counts[first + 2] = half - 1

    def deal(turn, carry):
        bucket = bucket_ref[turn]
        place = counts[bucket]
        late = jnp.logical_or(bucket == 2, bucket == 5)
        counts[bucket] = place + jnp.where(late, -1, 1)

        @pl.when(bucket < 3)
        def _():
            meta_keep[place] = meta_ref[turn]
            pltpu.make_async_copy(tiles.at[turn], keep.at[place], sem).start()

        @pl.when(bucket >= 3)
        def _():
            meta_send[place] = meta_ref[turn]
            pltpu.make_async_copy(tiles.at[turn], send.at[place], sem).start()

        return carry

    lax.fori_loop(0, total, deal, 0)
    pltpu.make_async_copy(tiles, tiles, sem).wait()


def pack(meta, bucket, tiles):
    half = tiles.shape[0] // 2
    block = jax.ShapeDtypeStruct((half,) + tiles.shape[1:], tiles.dtype)
    index = jax.ShapeDtypeStruct((half,), jnp.int32)
    return pl.pallas_call(
        pack_kernel,
        out_shape=(block, block, index, index),
        in_specs=[SMEM, SMEM, ANY],
        out_specs=(ANY, ANY, SMEM, SMEM),
        scratch_shapes=[pltpu.SMEM((8,), jnp.int32), pltpu.SemaphoreType.DMA],
        cost_estimate=pl.CostEstimate(flops=0, bytes_accessed=4 * tiles.size, transcendentals=0),
        name="pack",
    )(meta, bucket, tiles)


def load_band(pieces, band, sem):
    count = pieces[0].shape[0]
    return [
        pltpu.make_async_copy(piece, band.at[pl.ds(place * count, count)], sem.at[0])
        for place, piece in enumerate(pieces)
    ]


def add_tiles(meta_ref, first, count, tiles, band, acc, bits):
    mask = (1 << bits) - 1

    def add(turn, carry):
        meta = meta_ref[first + turn]
        row = lax.shift_right_logical(meta, bits)
        acc[row] += jnp.dot(
            tiles[turn], band[meta & mask], preferred_element_type=jnp.float32
        )
        return carry

    lax.fori_loop(0, count, add, 0, unroll=8)


def partial_kernel(bits, first, meta_keep, meta_recv, keep, recv, *rest):
    pieces, (out, band, mine, theirs, acc, sem) = rest[:6], rest[6:]
    count = mine.shape[0]
    copies = load_band(pieces, band, sem)
    copies.append(pltpu.make_async_copy(keep.at[pl.ds(first, count)], mine, sem.at[1]))
    copies.append(pltpu.make_async_copy(recv.at[pl.ds(first, count)], theirs, sem.at[2]))
    for copy in copies:
        copy.start()
    acc[...] = jnp.zeros_like(acc)
    pltpu.make_async_copy(band, band, sem.at[0]).wait()
    copies[6].wait()
    add_tiles(meta_keep, first, count, mine, band, acc, bits)
    copies[7].wait()
    add_tiles(meta_recv, first, count, theirs, band, acc, bits)
    out[...] = acc[...].astype(out.dtype)


def partial_sums(bits, meta_keep, meta_recv, keep, recv, pieces):
    count = keep.shape[0] // 2
    block = pieces[0].shape
    return pl.pallas_call(
        functools.partial(partial_kernel, bits, 0),
        out_shape=jax.ShapeDtypeStruct(block, jnp.bfloat16),
        in_specs=[SMEM, SMEM] + [ANY] * 8,
        out_specs=pl.BlockSpec(memory_space=pltpu.VMEM),
        scratch_shapes=[
            pltpu.VMEM((6 * block[0],) + block[1:], jnp.bfloat16),
            pltpu.VMEM((count,) + block[1:], jnp.bfloat16),
            pltpu.VMEM((count,) + block[1:], jnp.bfloat16),
            pltpu.VMEM(block, jnp.float32),
            pltpu.SemaphoreType.DMA((3,)),
        ],
        compiler_params=pltpu.CompilerParams(vmem_limit_bytes=48 * MIB),
        cost_estimate=pl.CostEstimate(
            flops=4 * count * block[1] * block[1] * block[2],
            bytes_accessed=22 * MIB,
            transcendentals=0,
        ),
        name="partial",
    )(meta_keep, meta_recv, keep, recv, *pieces)


def final_kernel(bits, first, meta_keep, meta_recv, places, keep, recv, inbox, other, *rest):
    pieces, (near, out, band, mine, theirs, inverse, acc, sem) = rest[:6], rest[6:]
    count = mine.shape[0]
    copies = load_band(pieces, band, sem)
    copies.append(pltpu.make_async_copy(keep.at[pl.ds(first, count)], mine, sem.at[1]))
    copies.append(pltpu.make_async_copy(recv.at[pl.ds(first, count)], theirs, sem.at[2]))
    copies.append(pltpu.make_async_copy(inbox, inverse, sem.at[3]))
    for copy in copies:
        copy.start()
    acc[...] = other[...].astype(jnp.float32)
    pltpu.make_async_copy(band, band, sem.at[0]).wait()
    copies[6].wait()
    add_tiles(meta_keep, first, count, mine, band, acc, bits)
    copies[7].wait()
    add_tiles(meta_recv, first, count, theirs, band, acc, bits)
    copies[8].wait()

    def apply(turn, carry):
        block = acc[turn].astype(jnp.bfloat16)
        near[turn] = block
        out[turn] = jnp.dot(
            inverse[places[turn]], block, preferred_element_type=jnp.float32
        ).astype(jnp.bfloat16)
        return carry

    lax.fori_loop(0, acc.shape[0], apply, 0, unroll=4)


def final(bits, meta_keep, meta_recv, places, keep, recv, inbox, other, pieces):
    count = keep.shape[0] // 2
    block = pieces[0].shape
    vmem = pl.BlockSpec(memory_space=pltpu.VMEM)
    result = jax.ShapeDtypeStruct(block, jnp.bfloat16)
    return pl.pallas_call(
        functools.partial(final_kernel, bits, count),
        out_shape=(result, result),
        in_specs=[SMEM] * 3 + [ANY] * 3 + [vmem] + [ANY] * 6,
        out_specs=(vmem, vmem),
        scratch_shapes=[
            pltpu.VMEM((6 * block[0],) + block[1:], jnp.bfloat16),
            pltpu.VMEM((count,) + block[1:], jnp.bfloat16),
            pltpu.VMEM((count,) + block[1:], jnp.bfloat16),
            pltpu.VMEM(inbox.shape, jnp.bfloat16),
            pltpu.VMEM(block, jnp.float32),
            pltpu.SemaphoreType.DMA((4,)),
        ],
        compiler_params=pltpu.CompilerParams(vmem_limit_bytes=48 * MIB),
        cost_estimate=pl.CostEstimate(
            flops=5 * count * block[1] * block[1] * block[2],
            bytes_accessed=28 * MIB,
            transcendentals=0,
        ),
        name="final",
    )(meta_keep, meta_recv, places, keep, recv, inbox, other, *pieces)


def ranks_within(labels):
    index = jnp.arange(labels.shape[0])
    same = labels[:, None] == labels[None, :]
    return jnp.sum((same & (index[:, None] > index[None, :])).astype(jnp.int32), axis=1)


def ranks_by(labels, key):
    same = labels[:, None] == labels[None, :]
    return jnp.sum((same & (key[:, None] > key[None, :])).astype(jnp.int32), axis=1)


def pick(values, wanted):
    position = jnp.arange(values.shape[0], dtype=jnp.int32)
    hit = wanted[:, None] == values[None, :]
    return jnp.sum(jnp.where(hit, position[None, :], 0), axis=1)


def per_device(rows, cols, sources, tiles, block_list, inverses, slot_cluster):
    size = tiles.shape[1]
    columns = sources.shape[1]
    own = sources.shape[0] // size
    devices = rows * cols
    half = cols // 2
    row = lax.axis_index("rows")
    col = lax.axis_index("cols")
    chip, core = col // 2, col % 2
    myself = row * cols + col
    blocks = sources.reshape(own, size, columns)

    def number(r, x, c):
        return r * cols + x * 2 + c

    def permute(value, pairs):
        return lax.ppermute(value, AXES, pairs)

    lines = [(x, c) for x in range(half) for c in range(2)]
    across = [
        (number(r, x, c), number(r, 1 - x, c)) for r in range(rows) for x, c in lines
    ]
    beside = [
        (number(r, x, c), number(r, x, 1 - c)) for r in range(rows) for x, c in lines
    ]
    up = [(r, r + 1) for r in range(rows - 1)]
    down = [(b, a) for a, b in up]
    early = [
        (number(a, x, c), number(b, x, c))
        for x, c in lines
        for a, b in (down if x == 0 else up)
    ]
    late = [
        (number(a, x, c), number(b, x, c))
        for x, c in lines
        for a, b in (up if x == 0 else down)
    ]

    other_chip = permute(blocks, across)
    halo_early = permute(blocks, early)
    own_beside = permute(blocks, beside)

    group = own * cols
    base = row * group
    bits = (8 * own - 1).bit_length()
    row_in = block_list[:, 0] - base
    owner = row_in // own
    column = block_list[:, 1] - base + group // 2
    quarter = column // own
    side = jnp.where(chip == 0, quarter // 2, 3 - quarter // 2)
    kind = (side + 3) % 4
    stays = owner % 2 == core
    reader = jnp.where(stays, core, 1 - core)
    slot = (jnp.minimum(kind, 2) * 2 + (quarter % 2 != reader)) * own + column % own
    meta = (row_in % own) * (1 << bits) + slot
    bucket = jnp.where(owner // 2 != chip, 0, jnp.where(kind == 3, 2, 1)) + jnp.where(stays, 0, 3)
    keep, send, meta_keep, meta_send = pack(meta, bucket, tiles)
    recv = permute(send, beside)
    meta_recv = permute(meta_send, beside)

    capacity = -(-own // devices)
    local = jnp.arange(own, dtype=jnp.int32)
    source = pick(slot_cluster, myself * own + local) // own
    places = source * capacity + ranks_by(source, local)
    held = lax.dynamic_slice_in_dim(slot_cluster, myself * own, own, 0)
    place_held = held // own * capacity + ranks_by(held // own, held % own)
    outbox = inverses[pick(place_held, jnp.arange(devices * capacity, dtype=jnp.int32))]
    inbox = lax.all_to_all(outbox, AXES, split_axis=0, concat_axis=0, tiled=True)

    other_beside = permute(other_chip, beside)
    halo_late = permute(other_chip, late)
    early_beside = permute(halo_early, beside)
    sums = partial_sums(
        bits,
        meta_keep,
        meta_recv,
        keep,
        recv,
        (blocks, own_beside, other_chip, other_beside, halo_early, early_beside),
    )
    other_sums = permute(sums, across)
    late_beside = permute(halo_late, beside)
    near, result = final(
        bits,
        meta_keep,
        meta_recv,
        places,
        keep,
        recv,
        inbox,
        other_sums,
        (blocks, own_beside, other_chip, other_beside, halo_late, late_beside),
    )
    return near.reshape(own * size, columns), result.reshape(own * size, columns)


def solution(mesh):
    spec = P(AXES, None)
    spec3 = P(AXES, None, None)
    return jax.shard_map(
        functools.partial(per_device, mesh.shape["rows"], mesh.shape["cols"]),
        mesh=mesh,
        in_specs=(spec, spec3, spec, spec3, P()),
        out_specs=(spec, spec),
        check_vma=False,
    )
```

```python
import functools

import jax
import jax.numpy as jnp
from jax import lax
from jax.experimental import pallas as pl
from jax.experimental.pallas import tpu as pltpu
from jax.sharding import PartitionSpec as P

AXES = ("rows", "cols")
MIB = 1024 * 1024
HBM = pl.BlockSpec(memory_space=pltpu.HBM)
SMEM = pl.BlockSpec(memory_space=pltpu.SMEM)
VMEM = pl.BlockSpec(memory_space=pltpu.VMEM)
CHUNK = 16


def params(mib):
    return pltpu.CompilerParams(vmem_limit_bytes=mib * MIB)


def cost(flops, mib):
    return pl.CostEstimate(flops=flops, bytes_accessed=mib * MIB, transcendentals=0)


def gather_kernel(first, order_ref, tiles, *rest):
    outs, (held, sem) = rest[:-2], rest[-2:]
    count = outs[0].shape[0]
    for part in range(len(outs)):

        def fetch(turn, carry):
            place = part * count + turn
            pltpu.make_async_copy(
                tiles.at[order_ref[first + place]], held.at[place], sem.at[part]
            ).start()
            return carry

        lax.fori_loop(0, count, fetch, 0, unroll=4)
    copies = []
    for part, out in enumerate(outs):
        block = held.at[pl.ds(part * count, count)]
        pltpu.make_async_copy(block, block, sem.at[part]).wait()
        copies.append(pltpu.make_async_copy(block, out, sem.at[len(outs) + part]))
        copies[-1].start()
    for copy in copies:
        copy.wait()


def gather_tiles(order, tiles, first, parts, name):
    count = tiles.shape[0] // 4
    block = (count,) + tiles.shape[1:]
    return pl.pallas_call(
        functools.partial(gather_kernel, first),
        out_shape=(jax.ShapeDtypeStruct(block, tiles.dtype),) * parts,
        in_specs=[SMEM, HBM],
        out_specs=(HBM,) * parts,
        scratch_shapes=[
            pltpu.VMEM((parts * count,) + tiles.shape[1:], tiles.dtype),
            pltpu.SemaphoreType.DMA((2 * parts,)),
        ],
        compiler_params=params(60),
        cost_estimate=cost(0, 8 * parts),
        name=name,
    )(order, tiles)


def add_tiles(meta_ref, place, count, tiles, start, band, acc, bits):
    mask = (1 << bits) - 1
    for turn in range(count):
        meta = meta_ref[place + turn]
        row = lax.shift_right_logical(meta, bits)
        acc[row] += jnp.dot(
            tiles[start + turn], band[meta & mask], preferred_element_type=jnp.float32
        )


def sums_kernel(bits, whole, meta_keep, meta_recv, bounds, keep, recv, *rest):
    count = keep.shape[0]
    pieces, (out, band, mine, theirs, acc, sem) = rest[:-6], rest[-6:]
    size = pieces[0].shape[0]
    loads = [
        pltpu.make_async_copy(piece, band.at[pl.ds(place * size, size)], sem.at[0])
        for place, piece in enumerate(pieces)
    ]
    loads.append(pltpu.make_async_copy(keep, mine, sem.at[1]))
    loads.append(pltpu.make_async_copy(recv, theirs, sem.at[2]))
    for load in loads:
        load.start()
    acc[...] = jnp.zeros_like(acc)
    pltpu.make_async_copy(band, band, sem.at[0]).wait()
    for side, (meta, held) in enumerate(((meta_keep, mine), (meta_recv, theirs))):
        loads[len(pieces) + side].wait()
        if whole:

            def add(turn, carry):
                add_tiles(meta, turn * CHUNK, CHUNK, held, turn * CHUNK, band, acc, bits)
                return carry

            lax.fori_loop(0, count // CHUNK, add, 0)
        else:

            def add_one(turn, carry):
                add_tiles(meta, turn, 1, held, turn, band, acc, bits)
                return carry

            end = bounds[side]
            even = end // 8 * 8

            def add_eight(turn, carry):
                add_tiles(meta, turn * 8, 8, held, turn * 8, band, acc, bits)
                return carry

            lax.fori_loop(0, end // 8, add_eight, 0)
            lax.fori_loop(even, end, add_one, 0)
    out[...] = acc[...].astype(out.dtype)


def sums(bits, whole, dtype, meta_keep, meta_recv, bounds, keep, recv, pieces, name):
    block = pieces[0].shape
    held = pltpu.VMEM(keep.shape, keep.dtype)
    return pl.pallas_call(
        functools.partial(sums_kernel, bits, whole),
        out_shape=jax.ShapeDtypeStruct(block, dtype),
        in_specs=[SMEM] * 3 + [HBM] * (2 + len(pieces)),
        out_specs=VMEM,
        scratch_shapes=[
            pltpu.VMEM((len(pieces) * block[0],) + block[1:], jnp.bfloat16),
            held,
            held,
            pltpu.VMEM(block, jnp.float32),
            pltpu.SemaphoreType.DMA((3,)),
        ],
        compiler_params=params(60),
        cost_estimate=cost(4 * keep.size * block[2], 24),
        name=name,
    )(meta_keep, meta_recv, bounds, keep, recv, *pieces)


def final_kernel(
    bits, meta_keep, meta_recv, bounds, places, early, other, keep, recv, late, beside, inbox, *rest
):
    near, out, acc, sent, band, mine, theirs, inverse, sem = rest
    count = keep.shape[0]
    size = late.shape[0]
    loads = [
        pltpu.make_async_copy(early, acc, sem.at[0]),
        pltpu.make_async_copy(other, sent, sem.at[1]),
        pltpu.make_async_copy(late, band.at[pl.ds(0, size)], sem.at[2]),
        pltpu.make_async_copy(beside, band.at[pl.ds(size, size)], sem.at[3]),
        pltpu.make_async_copy(inbox, inverse, sem.at[4]),
    ]
    for load in loads:
        load.start()
    sides = ((meta_keep, keep, mine), (meta_recv, recv, theirs))

    def chunk_copy(side, chunk):
        piece = pl.ds(pl.multiple_of(chunk * CHUNK, CHUNK), CHUNK)
        return pltpu.make_async_copy(sides[side][1].at[piece], sides[side][2].at[piece], sem.at[5 + side])

    for side in (0, 1):

        def fetch(chunk, carry):
            chunk_copy(side, chunk).start()
            return carry

        lax.fori_loop(bounds[side] // CHUNK, count // CHUNK, fetch, 0)
    for load in loads[:4]:
        load.wait()
    for side in (0, 1):

        def settle(chunk, carry):
            chunk_copy(side, chunk).wait()
            return carry

        lax.fori_loop(bounds[side] // CHUNK, count // CHUNK, settle, 0)
    for side, (meta_ref, keep_ref, held) in enumerate(sides):

        def add(turn, carry):
            meta = meta_ref[turn]
            row = lax.shift_right_logical(meta, bits)
            slot = (meta & ((1 << bits) - 1)) - 4 * size
            acc[row] += jnp.dot(held[turn], band[slot], preferred_element_type=jnp.float32)
            return carry

        def add_eight(turn, carry):
            for step in range(8):
                add(turn * 8 + step, carry)
            return carry

        first = bounds[side]
        even = (first + 7) // 8
        lax.fori_loop(first, even * 8, add, 0)
        lax.fori_loop(even, count // 8, add_eight, 0)
    loads[4].wait()

    def apply(turn, carry):
        block = (acc[turn] + sent[turn].astype(jnp.float32)).astype(jnp.bfloat16)
        near[turn] = block
        out[turn] = jnp.dot(
            inverse[places[turn]], block, preferred_element_type=jnp.float32
        ).astype(jnp.bfloat16)
        return carry

    lax.fori_loop(0, size, apply, 0, unroll=8)


def final(bits, meta_keep, meta_recv, bounds, places, early, other, keep, recv, late, beside, inbox):
    block = late.shape
    held = pltpu.VMEM(keep.shape, keep.dtype)
    result = jax.ShapeDtypeStruct(block, jnp.bfloat16)
    return pl.pallas_call(
        functools.partial(final_kernel, bits),
        out_shape=(result, result),
        in_specs=[SMEM] * 4 + [HBM] * 7,
        out_specs=(VMEM, VMEM),
        scratch_shapes=[
            pltpu.VMEM(block, jnp.float32),
            pltpu.VMEM(block, jnp.bfloat16),
            pltpu.VMEM((2 * block[0],) + block[1:], jnp.bfloat16),
            held,
            held,
            pltpu.VMEM(inbox.shape, jnp.bfloat16),
            pltpu.SemaphoreType.DMA((7,)),
        ],
        compiler_params=params(60),
        cost_estimate=cost(3 * keep.size * block[2], 20),
        name="final",
    )(meta_keep, meta_recv, bounds, places, early, other, keep, recv, late, beside, inbox)


def ranks_by(labels, key):
    same = labels[:, None] == labels[None, :]
    return jnp.sum((same & (key[:, None] > key[None, :])).astype(jnp.int32), axis=1)


def pick(values, wanted):
    position = jnp.arange(values.shape[0], dtype=jnp.int32)
    hit = wanted[:, None] == values[None, :]
    return jnp.sum(jnp.where(hit, position[None, :], 0), axis=1)


def per_device(rows, cols, sources, tiles, block_list, inverses, slot_cluster):
    size = tiles.shape[1]
    columns = sources.shape[1]
    own = sources.shape[0] // size
    devices = rows * cols
    half = cols // 2
    row = lax.axis_index("rows")
    col = lax.axis_index("cols")
    chip, core = col // 2, col % 2
    myself = row * cols + col
    blocks = sources.reshape(own, size, columns)

    def number(r, x, c):
        return r * cols + x * 2 + c

    def permute(value, pairs):
        return lax.ppermute(value, AXES, pairs)

    lines = [(x, c) for x in range(half) for c in range(2)]
    across = [
        (number(r, x, c), number(r, 1 - x, c)) for r in range(rows) for x, c in lines
    ]
    beside = [
        (number(r, x, c), number(r, x, 1 - c)) for r in range(rows) for x, c in lines
    ]
    up = [(r, r + 1) for r in range(rows - 1)]
    down = [(b, a) for a, b in up]
    early = [
        (number(a, x, c), number(b, x, c))
        for x, c in lines
        for a, b in (down if x == 0 else up)
    ]
    late = [
        (number(a, x, c), number(b, x, c))
        for x, c in lines
        for a, b in (up if x == 0 else down)
    ]

    other_chip = permute(blocks, across)
    halo_early = permute(blocks, early)
    own_beside = permute(blocks, beside)

    group = own * cols
    base = row * group
    bits = (8 * own - 1).bit_length()
    row_in = block_list[:, 0] - base
    owner = row_in // own
    column = block_list[:, 1] - base + group // 2
    quarter = column // own
    side = jnp.where(chip == 0, quarter // 2, 3 - quarter // 2)
    kind = (side + 3) % 4
    stays = owner % 2 == core
    reader = jnp.where(stays, core, 1 - core)
    slot = (jnp.minimum(kind, 2) * 2 + (quarter % 2 != reader)) * own + column % own
    meta = (row_in % own) * (1 << bits) + slot
    bucket = jnp.where(owner // 2 != chip, 0, jnp.where(kind == 3, 2, 1)) + jnp.where(stays, 0, 3)
    total = tiles.shape[0]
    quarter_count = total // 4
    index = jnp.arange(total, dtype=jnp.int32)
    key = bucket * total + index
    rank = jnp.sum((key[:, None] > key[None, :]).astype(jnp.int32), axis=1)
    placed = rank[None, :] == index[:, None]
    order = jnp.sum(jnp.where(placed, index[None, :], 0), axis=1)
    meta = jnp.sum(jnp.where(placed, meta[None, :], 0), axis=1)
    bound_keep = jnp.sum((bucket == 1).astype(jnp.int32), keepdims=True)
    bound_send = jnp.sum((bucket == 4).astype(jnp.int32), keepdims=True)
    padding = jnp.zeros((127,), jnp.int32)
    send_cross, send_own = gather_tiles(order, tiles, 2 * quarter_count, 2, "pack_send")
    recv_cross = permute(send_cross, beside)
    recv_own = permute(send_own, beside)
    meta_recv = permute(
        jnp.concatenate([meta[2 * quarter_count :], bound_send, padding]), beside
    )
    keep_cross, keep_own = gather_tiles(order, tiles, 0, 2, "pack_keep")
    bounds = jnp.concatenate([bound_keep, meta_recv[2 * quarter_count : 2 * quarter_count + 1]])

    capacity = -(-own // devices)
    local = jnp.arange(own, dtype=jnp.int32)
    source = pick(slot_cluster, myself * own + local) // own
    places = source * capacity + ranks_by(source, local)
    held = lax.dynamic_slice_in_dim(slot_cluster, myself * own, own, 0)
    place_held = held // own * capacity + ranks_by(held // own, held % own)
    outbox = inverses[pick(place_held, jnp.arange(devices * capacity, dtype=jnp.int32))]
    inbox = lax.all_to_all(outbox, AXES, split_axis=0, concat_axis=0, tiled=True)

    other_beside = permute(other_chip, beside)
    halo_late = permute(other_chip, late)
    early_beside = permute(halo_early, beside)
    group_pieces = (blocks, own_beside, other_chip, other_beside)
    cross = sums(
        bits,
        True,
        jnp.bfloat16,
        meta[:quarter_count],
        meta_recv[:quarter_count],
        bounds,
        keep_cross,
        recv_cross,
        group_pieces + (halo_early, early_beside),
        "cross",
    )
    other_sums = permute(cross, across)
    own_keep = meta[quarter_count : 2 * quarter_count]
    own_recv = meta_recv[quarter_count : 2 * quarter_count]
    early_sums = sums(
        bits,
        False,
        jnp.float32,
        own_keep,
        own_recv,
        bounds,
        keep_own,
        recv_own,
        group_pieces,
        "own",
    )
    halo_late, early_sums = lax.optimization_barrier((halo_late, early_sums))
    late_beside = permute(halo_late, beside)
    near, result = final(
        bits,
        own_keep,
        own_recv,
        bounds,
        places,
        early_sums,
        other_sums,
        keep_own,
        recv_own,
        halo_late,
        late_beside,
        inbox,
    )
    return near.reshape(own * size, columns), result.reshape(own * size, columns)


def solution(mesh):
    spec = P(AXES, None)
    spec3 = P(AXES, None, None)
    return jax.shard_map(
        functools.partial(per_device, mesh.shape["rows"], mesh.shape["cols"]),
        mesh=mesh,
        in_specs=(spec, spec3, spec, spec3, P()),
        out_specs=(spec, spec),
        check_vma=False,
    )
```

```python
import functools

import jax
import jax.numpy as jnp
from jax import lax
from jax.experimental import pallas as pl
from jax.experimental.pallas import tpu as pltpu
from jax.sharding import PartitionSpec as P

AXES = ("rows", "cols")
MIB = 1024 * 1024
HBM = pl.BlockSpec(memory_space=pltpu.HBM)
SMEM = pl.BlockSpec(memory_space=pltpu.SMEM)
VMEM = pl.BlockSpec(memory_space=pltpu.VMEM)
CHUNK = 16


def params(mib):
    return pltpu.CompilerParams(vmem_limit_bytes=mib * MIB)


def cost(flops, mib):
    return pl.CostEstimate(flops=flops, bytes_accessed=mib * MIB, transcendentals=0)


def gather_kernel(first, order_ref, tiles, *rest):
    outs, (held, sem) = rest[:-2], rest[-2:]
    count = outs[0].shape[0]
    for part in range(len(outs)):

        def fetch(turn, carry):
            place = part * count + turn
            pltpu.make_async_copy(
                tiles.at[order_ref[first + place]], held.at[place], sem.at[part]
            ).start()
            return carry

        lax.fori_loop(0, count, fetch, 0, unroll=4)
    copies = []
    for part, out in enumerate(outs):
        block = held.at[pl.ds(part * count, count)]
        pltpu.make_async_copy(block, block, sem.at[part]).wait()
        copies.append(pltpu.make_async_copy(block, out, sem.at[len(outs) + part]))
        copies[-1].start()
    for copy in copies:
        copy.wait()


def gather_tiles(order, tiles, first, parts, name):
    count = tiles.shape[0] // 4
    block = (count,) + tiles.shape[1:]
    return pl.pallas_call(
        functools.partial(gather_kernel, first),
        out_shape=(jax.ShapeDtypeStruct(block, tiles.dtype),) * parts,
        in_specs=[SMEM, HBM],
        out_specs=(HBM,) * parts,
        scratch_shapes=[
            pltpu.VMEM((parts * count,) + tiles.shape[1:], tiles.dtype),
            pltpu.SemaphoreType.DMA((2 * parts,)),
        ],
        compiler_params=params(60),
        cost_estimate=cost(0, 8 * parts),
        name=name,
    )(order, tiles)


def add_tiles(meta_ref, place, count, tiles, start, band, acc, bits):
    mask = (1 << bits) - 1
    for turn in range(count):
        meta = meta_ref[place + turn]
        row = lax.shift_right_logical(meta, bits)
        acc[row] += jnp.dot(
            tiles[start + turn], band[meta & mask], preferred_element_type=jnp.float32
        )


def sums_kernel(bits, whole, meta_keep, meta_recv, bounds, keep, recv, *rest):
    count = keep.shape[0]
    pieces, (out, band, mine, theirs, acc, sem) = rest[:-6], rest[-6:]
    size = pieces[0].shape[0]
    loads = [
        pltpu.make_async_copy(piece, band.at[pl.ds(place * size, size)], sem.at[0])
        for place, piece in enumerate(pieces)
    ]
    loads.append(pltpu.make_async_copy(keep, mine, sem.at[1]))
    loads.append(pltpu.make_async_copy(recv, theirs, sem.at[2]))
    for load in loads:
        load.start()
    acc[...] = jnp.zeros_like(acc)
    pltpu.make_async_copy(band, band, sem.at[0]).wait()
    for side, (meta, held) in enumerate(((meta_keep, mine), (meta_recv, theirs))):
        loads[len(pieces) + side].wait()
        if whole:

            def add(turn, carry):
                add_tiles(meta, turn * CHUNK, CHUNK, held, turn * CHUNK, band, acc, bits)
                return carry

            lax.fori_loop(0, count // CHUNK, add, 0)
        else:

            def add_one(turn, carry):
                add_tiles(meta, turn, 1, held, turn, band, acc, bits)
                return carry

            end = bounds[side]
            even = end // 8 * 8

            def add_eight(turn, carry):
                add_tiles(meta, turn * 8, 8, held, turn * 8, band, acc, bits)
                return carry

            lax.fori_loop(0, end // 8, add_eight, 0)
            lax.fori_loop(even, end, add_one, 0)
    out[...] = acc[...].astype(out.dtype)


def sums(bits, whole, dtype, meta_keep, meta_recv, bounds, keep, recv, pieces, name):
    block = pieces[0].shape
    held = pltpu.VMEM(keep.shape, keep.dtype)
    return pl.pallas_call(
        functools.partial(sums_kernel, bits, whole),
        out_shape=jax.ShapeDtypeStruct(block, dtype),
        in_specs=[SMEM] * 3 + [HBM] * (2 + len(pieces)),
        out_specs=VMEM,
        scratch_shapes=[
            pltpu.VMEM((len(pieces) * block[0],) + block[1:], jnp.bfloat16),
            held,
            held,
            pltpu.VMEM(block, jnp.float32),
            pltpu.SemaphoreType.DMA((3,)),
        ],
        compiler_params=params(60),
        cost_estimate=cost(4 * keep.size * block[2], 24),
        name=name,
    )(meta_keep, meta_recv, bounds, keep, recv, *pieces)


def final_kernel(
    bits, meta_keep, meta_recv, bounds, places, early, other, keep, recv, late, beside, inbox, *rest
):
    near, out, acc, sent, band, mine, theirs, inverse, sem = rest
    count = keep.shape[0]
    size = late.shape[0]
    loads = [
        pltpu.make_async_copy(early, acc, sem.at[0]),
        pltpu.make_async_copy(other, sent, sem.at[1]),
        pltpu.make_async_copy(late, band.at[pl.ds(0, size)], sem.at[2]),
        pltpu.make_async_copy(beside, band.at[pl.ds(size, size)], sem.at[3]),
        pltpu.make_async_copy(inbox, inverse, sem.at[4]),
    ]
    for load in loads:
        load.start()
    sides = ((meta_keep, keep, mine), (meta_recv, recv, theirs))

    def chunk_copy(side, chunk):
        piece = pl.ds(pl.multiple_of(chunk * CHUNK, CHUNK), CHUNK)
        return pltpu.make_async_copy(sides[side][1].at[piece], sides[side][2].at[piece], sem.at[5 + side])

    for side in (0, 1):

        def fetch(chunk, carry):
            chunk_copy(side, chunk).start()
            return carry

        lax.fori_loop(bounds[side] // CHUNK, count // CHUNK, fetch, 0)
    for load in loads[:4]:
        load.wait()
    for side in (0, 1):

        def settle(chunk, carry):
            chunk_copy(side, chunk).wait()
            return carry

        lax.fori_loop(bounds[side] // CHUNK, count // CHUNK, settle, 0)
    for side, (meta_ref, keep_ref, held) in enumerate(sides):

        def add(turn, carry):
            meta = meta_ref[turn]
            row = lax.shift_right_logical(meta, bits)
            slot = (meta & ((1 << bits) - 1)) - 4 * size
            acc[row] += jnp.dot(held[turn], band[slot], preferred_element_type=jnp.float32)
            return carry

        def add_eight(turn, carry):
            for step in range(8):
                add(turn * 8 + step, carry)
            return carry

        first = bounds[side]
        even = (first + 7) // 8
        lax.fori_loop(first, even * 8, add, 0)
        lax.fori_loop(even, count // 8, add_eight, 0)
    loads[4].wait()

    def apply(turn, carry):
        block = (acc[turn] + sent[turn].astype(jnp.float32)).astype(jnp.bfloat16)
        near[turn] = block
        out[turn] = jnp.dot(
            inverse[places[turn]], block, preferred_element_type=jnp.float32
        ).astype(jnp.bfloat16)
        return carry

    lax.fori_loop(0, size, apply, 0, unroll=8)


def final(bits, meta_keep, meta_recv, bounds, places, early, other, keep, recv, late, beside, inbox):
    block = late.shape
    held = pltpu.VMEM(keep.shape, keep.dtype)
    result = jax.ShapeDtypeStruct(block, jnp.bfloat16)
    return pl.pallas_call(
        functools.partial(final_kernel, bits),
        out_shape=(result, result),
        in_specs=[SMEM] * 4 + [HBM] * 7,
        out_specs=(VMEM, VMEM),
        scratch_shapes=[
            pltpu.VMEM(block, jnp.float32),
            pltpu.VMEM(block, jnp.bfloat16),
            pltpu.VMEM((2 * block[0],) + block[1:], jnp.bfloat16),
            held,
            held,
            pltpu.VMEM(inbox.shape, jnp.bfloat16),
            pltpu.SemaphoreType.DMA((7,)),
        ],
        compiler_params=params(60),
        cost_estimate=cost(3 * keep.size * block[2], 20),
        name="final",
    )(meta_keep, meta_recv, bounds, places, early, other, keep, recv, late, beside, inbox)


def ranks_by(labels, key):
    same = labels[:, None] == labels[None, :]
    return jnp.sum((same & (key[:, None] > key[None, :])).astype(jnp.int32), axis=1)


def pick(values, wanted):
    position = jnp.arange(values.shape[0], dtype=jnp.int32)
    hit = wanted[:, None] == values[None, :]
    return jnp.sum(jnp.where(hit, position[None, :], 0), axis=1)


def per_device(rows, cols, sources, tiles, block_list, inverses, slot_cluster):
    size = tiles.shape[1]
    columns = sources.shape[1]
    own = sources.shape[0] // size
    devices = rows * cols
    half = cols // 2
    row = lax.axis_index("rows")
    col = lax.axis_index("cols")
    chip, core = col // 2, col % 2
    myself = row * cols + col
    blocks = sources.reshape(own, size, columns)

    def number(r, x, c):
        return r * cols + x * 2 + c

    def permute(value, pairs):
        return lax.ppermute(value, AXES, pairs)

    lines = [(x, c) for x in range(half) for c in range(2)]
    across = [
        (number(r, x, c), number(r, 1 - x, c)) for r in range(rows) for x, c in lines
    ]
    beside = [
        (number(r, x, c), number(r, x, 1 - c)) for r in range(rows) for x, c in lines
    ]
    up = [(r, r + 1) for r in range(rows - 1)]
    down = [(b, a) for a, b in up]
    early = [
        (number(a, x, c), number(b, x, c))
        for x, c in lines
        for a, b in (down if x == 0 else up)
    ]
    late = [
        (number(a, x, c), number(b, x, c))
        for x, c in lines
        for a, b in (up if x == 0 else down)
    ]

    other_chip = permute(blocks, across)
    halo_early = permute(blocks, early)
    own_beside = permute(blocks, beside)

    group = own * cols
    base = row * group
    bits = (8 * own - 1).bit_length()
    row_in = block_list[:, 0] - base
    owner = row_in // own
    column = block_list[:, 1] - base + group // 2
    quarter = column // own
    side = jnp.where(chip == 0, quarter // 2, 3 - quarter // 2)
    kind = (side + 3) % 4
    stays = owner % 2 == core
    reader = jnp.where(stays, core, 1 - core)
    slot = (jnp.minimum(kind, 2) * 2 + (quarter % 2 != reader)) * own + column % own
    meta = (row_in % own) * (1 << bits) + slot
    bucket = jnp.where(owner // 2 != chip, 0, jnp.where(kind == 3, 2, 1)) + jnp.where(stays, 0, 3)
    total = tiles.shape[0]
    quarter_count = total // 4
    index = jnp.arange(total, dtype=jnp.int32)
    key = bucket * total + index
    rank = jnp.sum((key[:, None] > key[None, :]).astype(jnp.int32), axis=1)
    placed = rank[None, :] == index[:, None]
    order = jnp.sum(jnp.where(placed, index[None, :], 0), axis=1)
    meta = jnp.sum(jnp.where(placed, meta[None, :], 0), axis=1)
    bound_keep = jnp.sum((bucket == 1).astype(jnp.int32), keepdims=True)
    bound_send = jnp.sum((bucket == 4).astype(jnp.int32), keepdims=True)
    padding = jnp.zeros((127,), jnp.int32)
    send_cross, send_own = gather_tiles(order, tiles, 2 * quarter_count, 2, "pack_send")
    recv_cross = permute(send_cross, beside)
    recv_own = permute(send_own, beside)
    meta_recv = permute(
        jnp.concatenate([meta[2 * quarter_count :], bound_send, padding]), beside
    )
    keep_cross, keep_own = gather_tiles(order, tiles, 0, 2, "pack_keep")
    bounds = jnp.concatenate([bound_keep, meta_recv[2 * quarter_count : 2 * quarter_count + 1]])

    capacity = -(-own // devices)
    local = jnp.arange(own, dtype=jnp.int32)
    source = pick(slot_cluster, myself * own + local) // own
    places = source * capacity + ranks_by(source, local)
    held = lax.dynamic_slice_in_dim(slot_cluster, myself * own, own, 0)
    place_held = held // own * capacity + ranks_by(held // own, held % own)
    outbox = inverses[pick(place_held, jnp.arange(devices * capacity, dtype=jnp.int32))]

    own_keep = meta[quarter_count : 2 * quarter_count]
    own_recv = meta_recv[quarter_count : 2 * quarter_count]
    cross_keep = meta[:quarter_count]
    cross_recv = meta_recv[:quarter_count]
    (
        other_chip,
        halo_early,
        keep_cross,
        keep_own,
        outbox,
        bounds,
        own_keep,
        own_recv,
        cross_keep,
        cross_recv,
        places,
    ) = lax.optimization_barrier(
        (
            other_chip,
            halo_early,
            keep_cross,
            keep_own,
            outbox,
            bounds,
            own_keep,
            own_recv,
            cross_keep,
            cross_recv,
            places,
        )
    )
    inbox = lax.all_to_all(outbox, AXES, split_axis=0, concat_axis=0, tiled=True)

    other_beside = permute(other_chip, beside)
    halo_late = permute(other_chip, late)
    early_beside = permute(halo_early, beside)
    group_pieces = (blocks, own_beside, other_chip, other_beside)
    cross = sums(
        bits,
        True,
        jnp.bfloat16,
        cross_keep,
        cross_recv,
        bounds,
        keep_cross,
        recv_cross,
        group_pieces + (halo_early, early_beside),
        "cross",
    )
    other_sums = permute(cross, across)
    early_sums = sums(
        bits,
        False,
        jnp.float32,
        own_keep,
        own_recv,
        bounds,
        keep_own,
        recv_own,
        group_pieces,
        "own",
    )
    halo_late, early_sums = lax.optimization_barrier((halo_late, early_sums))
    late_beside = permute(halo_late, beside)
    near, result = final(
        bits,
        own_keep,
        own_recv,
        bounds,
        places,
        early_sums,
        other_sums,
        keep_own,
        recv_own,
        halo_late,
        late_beside,
        inbox,
    )
    return near.reshape(own * size, columns), result.reshape(own * size, columns)


def solution(mesh):
    spec = P(AXES, None)
    spec3 = P(AXES, None, None)
    return jax.shard_map(
        functools.partial(per_device, mesh.shape["rows"], mesh.shape["cols"]),
        mesh=mesh,
        in_specs=(spec, spec3, spec, spec3, P()),
        out_specs=(spec, spec),
        check_vma=False,
    )
```

```python
import functools
import math

import jax
import jax.numpy as jnp
from jax import lax
from jax.experimental import pallas as pl
from jax.experimental.pallas import tpu as pltpu
from jax.sharding import PartitionSpec as P

AXES = ("rows", "cols")
MIB = 1024 * 1024
HBM = pl.BlockSpec(memory_space=pltpu.HBM)
SMEM = pl.BlockSpec(memory_space=pltpu.SMEM)
VMEM = pl.BlockSpec(memory_space=pltpu.VMEM)
CHUNK = 16


def params(mib):
    return pltpu.CompilerParams(vmem_limit_bytes=mib * MIB)


def cost(flops, mib):
    return pl.CostEstimate(flops=flops, bytes_accessed=mib * MIB, transcendentals=0)


def gather_kernel(first, order_ref, tiles, *rest):
    outs, (held, sem) = rest[:-2], rest[-2:]
    parts = len(outs)
    count = outs[0].shape[0]
    for part in range(parts):

        def fetch(turn, carry):
            place = part * count + turn
            pltpu.make_async_copy(
                tiles.at[order_ref[first + place]], held.at[place], sem.at[part]
            ).start()
            return carry

        lax.fori_loop(0, count, fetch, 0, unroll=4)
    copies = []
    for part, out in enumerate(outs):
        block = held.at[pl.ds(part * count, count)]
        pltpu.make_async_copy(block, block, sem.at[part]).wait()
        copies.append(pltpu.make_async_copy(block, out, sem.at[parts + part]))
        copies[-1].start()
    for copy in copies:
        copy.wait()


def gather_tiles(order, tiles, first, parts, count, name):
    block = (count,) + tiles.shape[1:]
    return pl.pallas_call(
        functools.partial(gather_kernel, first),
        out_shape=(jax.ShapeDtypeStruct(block, tiles.dtype),) * parts,
        in_specs=[SMEM, HBM],
        out_specs=(HBM,) * parts,
        scratch_shapes=[
            pltpu.VMEM((parts * count,) + tiles.shape[1:], tiles.dtype),
            pltpu.SemaphoreType.DMA((2 * parts,)),
        ],
        compiler_params=params(63),
        cost_estimate=pl.CostEstimate(
            flops=0, bytes_accessed=8 * parts * math.prod(block), transcendentals=0
        ),
        name=name,
    )(order, tiles)


def add_tiles(meta_ref, place, count, tiles, start, band, acc, bits):
    mask = (1 << bits) - 1
    for turn in range(count):
        meta = meta_ref[place + turn]
        row = lax.shift_right_logical(meta, bits)
        acc[row] += jnp.dot(
            tiles[start + turn], band[meta & mask], preferred_element_type=jnp.float32
        )


def sums_kernel(bits, whole, meta_keep, meta_recv, bounds, keep, recv, *rest):
    count = keep.shape[0]
    pieces, (out, band, mine, theirs, acc, sem) = rest[:-6], rest[-6:]
    size = pieces[0].shape[0]
    loads = [
        pltpu.make_async_copy(part, band.at[pl.ds(place * size, size)], sem.at[0])
        for place, part in enumerate(pieces)
    ]
    loads.append(pltpu.make_async_copy(keep, mine, sem.at[1]))
    loads.append(pltpu.make_async_copy(recv, theirs, sem.at[2]))
    for load in loads:
        load.start()
    acc[...] = jnp.zeros_like(acc)
    pltpu.make_async_copy(band, band, sem.at[0]).wait()
    for side, (meta, held) in enumerate(((meta_keep, mine), (meta_recv, theirs))):
        loads[len(pieces) + side].wait()
        if whole:

            def add(turn, carry):
                add_tiles(meta, turn * CHUNK, CHUNK, held, turn * CHUNK, band, acc, bits)
                return carry

            lax.fori_loop(0, count // CHUNK, add, 0)
        else:

            def add_one(turn, carry):
                add_tiles(meta, turn, 1, held, turn, band, acc, bits)
                return carry

            end = bounds[side]
            even = end // 8 * 8

            def add_eight(turn, carry):
                add_tiles(meta, turn * 8, 8, held, turn * 8, band, acc, bits)
                return carry

            lax.fori_loop(0, end // 8, add_eight, 0)
            lax.fori_loop(even, end, add_one, 0)
    out[...] = acc[...].astype(out.dtype)


def sums(bits, whole, dtype, meta_keep, meta_recv, bounds, keep, recv, pieces, name):
    block = pieces[0].shape
    held = pltpu.VMEM(keep.shape, keep.dtype)
    return pl.pallas_call(
        functools.partial(sums_kernel, bits, whole),
        out_shape=jax.ShapeDtypeStruct(block, dtype),
        in_specs=[SMEM] * 3 + [HBM] * (2 + len(pieces)),
        out_specs=VMEM,
        scratch_shapes=[
            pltpu.VMEM((len(pieces) * block[0],) + block[1:], jnp.bfloat16),
            held,
            held,
            pltpu.VMEM(block, jnp.float32),
            pltpu.SemaphoreType.DMA((3,)),
        ],
        compiler_params=params(63),
        cost_estimate=cost(4 * keep.size * block[2], 24),
        name=name,
    )(meta_keep, meta_recv, bounds, keep, recv, *pieces)


def near_kernel(bits, meta_keep, meta_recv, bounds, early, other, keep, recv, late, beside, *rest):
    near, acc, sent, band, mine, theirs, sem = rest
    count = keep.shape[0]
    size = late.shape[0]
    loads = [
        pltpu.make_async_copy(early, acc, sem.at[0]),
        pltpu.make_async_copy(late, band.at[pl.ds(0, size)], sem.at[2]),
        pltpu.make_async_copy(beside, band.at[pl.ds(size, size)], sem.at[3]),
        pltpu.make_async_copy(other, sent, sem.at[1]),
    ]
    for load in loads:
        load.start()
    sides = ((meta_keep, keep, mine), (meta_recv, recv, theirs))

    def chunk_copy(side, chunk):
        start = pl.multiple_of(chunk * CHUNK, CHUNK)
        piece = pl.ds(start, CHUNK)
        return pltpu.make_async_copy(
            sides[side][1].at[piece], sides[side][2].at[piece], sem.at[4 + side]
        )

    for side in (0, 1):

        def fetch(chunk, carry):
            chunk_copy(side, chunk).start()
            return carry

        lax.fori_loop(bounds[side] // CHUNK, count // CHUNK, fetch, 0)
    for side in (0, 1):

        def settle(chunk, carry):
            chunk_copy(side, chunk).wait()
            return carry

        lax.fori_loop(bounds[side] // CHUNK, count // CHUNK, settle, 0)
    for load in loads:
        load.wait()
    for side, (meta_ref, keep_ref, held) in enumerate(sides):

        def add(turn, carry):
            meta = meta_ref[turn]
            row = lax.shift_right_logical(meta, bits)
            slot = (meta & ((1 << bits) - 1)) - 4 * size
            acc[row] += jnp.dot(held[turn], band[slot], preferred_element_type=jnp.float32)
            return carry

        def add_eight(turn, carry):
            for step in range(8):
                add(turn * 8 + step, carry)
            return carry

        first = bounds[side]
        even = (first + 7) // 8
        lax.fori_loop(first, even * 8, add, 0)
        lax.fori_loop(even, count // 8, add_eight, 0)
    near[...] = (acc[...] + sent[...].astype(jnp.float32)).astype(jnp.bfloat16)


def near_sums(bits, meta_keep, meta_recv, bounds, early, other, keep, recv, late, beside):
    block = late.shape
    held = pltpu.VMEM(keep.shape, keep.dtype)
    return pl.pallas_call(
        functools.partial(near_kernel, bits),
        out_shape=jax.ShapeDtypeStruct(block, jnp.bfloat16),
        in_specs=[SMEM] * 3 + [HBM] * 6,
        out_specs=VMEM,
        scratch_shapes=[
            pltpu.VMEM(block, jnp.float32),
            pltpu.VMEM(block, jnp.bfloat16),
            pltpu.VMEM((2 * block[0],) + block[1:], jnp.bfloat16),
            held,
            held,
            pltpu.SemaphoreType.DMA((6,)),
        ],
        compiler_params=params(63),
        cost_estimate=cost(2 * keep.size * block[2], 18),
        name="near",
    )(meta_keep, meta_recv, bounds, early, other, keep, recv, late, beside)


def apply_kernel(places, near, *rest):
    inbox, (out, inverse, sem) = rest[:-3], rest[-3:]
    loads = []
    for place, part in enumerate(inbox):
        count = part.shape[0]
        loads.append(
            pltpu.make_async_copy(part, inverse.at[pl.ds(place * count, count)], sem.at[place])
        )
        loads[-1].start()
    for load in loads:
        load.wait()

    def apply(turn, carry):
        out[turn] = jnp.dot(
            inverse[places[turn]], near[turn], preferred_element_type=jnp.float32
        ).astype(jnp.bfloat16)
        return carry

    lax.fori_loop(0, near.shape[0], apply, 0, unroll=16)


def apply_inverses(places, near, inbox):
    block = inbox[0].shape
    return pl.pallas_call(
        apply_kernel,
        out_shape=jax.ShapeDtypeStruct(near.shape, jnp.bfloat16),
        in_specs=[SMEM, VMEM] + [HBM] * len(inbox),
        out_specs=VMEM,
        scratch_shapes=[
            pltpu.VMEM((len(inbox) * block[0],) + block[1:], jnp.bfloat16),
            pltpu.SemaphoreType.DMA((len(inbox),)),
        ],
        compiler_params=params(63),
        cost_estimate=cost(2 * near.size * near.shape[1], 6),
        name="apply",
    )(places, near, *inbox)


def ranks_by(labels, key):
    same = labels[:, None] == labels[None, :]
    return jnp.sum((same & (key[:, None] > key[None, :])).astype(jnp.int32), axis=1)


def pick(values, wanted):
    position = jnp.arange(values.shape[0], dtype=jnp.int32)
    hit = wanted[:, None] == values[None, :]
    return jnp.sum(jnp.where(hit, position[None, :], 0), axis=1)


def per_device(rows, cols, sources, tiles, block_list, inverses, slot_cluster):
    size = tiles.shape[1]
    columns = sources.shape[1]
    own = sources.shape[0] // size
    devices = rows * cols
    half = cols // 2
    row = lax.axis_index("rows")
    col = lax.axis_index("cols")
    chip, core = col // 2, col % 2
    myself = row * cols + col
    blocks = sources.reshape(own, size, columns)

    def number(r, x, c):
        return r * cols + x * 2 + c

    def permute(value, pairs):
        return lax.ppermute(value, AXES, pairs)

    lines = [(x, c) for x in range(half) for c in range(2)]
    across = [
        (number(r, x, c), number(r, 1 - x, c)) for r in range(rows) for x, c in lines
    ]
    beside = [
        (number(r, x, c), number(r, x, 1 - c)) for r in range(rows) for x, c in lines
    ]
    up = [(r, r + 1) for r in range(rows - 1)]
    down = [(b, a) for a, b in up]
    early = [
        (number(a, x, c), number(b, x, c))
        for x, c in lines
        for a, b in (down if x == 0 else up)
    ]
    late = [
        (number(a, x, c), number(b, x, c))
        for x, c in lines
        for a, b in (up if x == 0 else down)
    ]

    other_chip = permute(blocks, across)
    halo_early = permute(blocks, early)
    own_beside = permute(blocks, beside)

    capacity = -(-own // devices)
    local = jnp.arange(own, dtype=jnp.int32)
    source = pick(slot_cluster, myself * own + local) // own
    places = ranks_by(source, local) * devices + source
    held = lax.dynamic_slice_in_dim(slot_cluster, myself * own, own, 0)
    target = held // own
    place_held = ranks_by(target, held % own) * devices + target
    outbox_order = pick(place_held, jnp.arange(devices * capacity, dtype=jnp.int32))
    outbox = gather_tiles(outbox_order, inverses, 0, capacity, devices, "pack_inverses")

    def exchange(value):
        return lax.all_to_all(value, AXES, split_axis=0, concat_axis=0, tiled=True)

    inbox = [exchange(outbox[0])]

    group = own * cols
    base = row * group
    bits = (8 * own - 1).bit_length()
    row_in = block_list[:, 0] - base
    owner = row_in // own
    column = block_list[:, 1] - base + group // 2
    quarter = column // own
    side = jnp.where(chip == 0, quarter // 2, 3 - quarter // 2)
    kind = (side + 3) % 4
    stays = owner % 2 == core
    reader = jnp.where(stays, core, 1 - core)
    slot = (jnp.minimum(kind, 2) * 2 + (quarter % 2 != reader)) * own + column % own
    meta = (row_in % own) * (1 << bits) + slot
    bucket = jnp.where(owner // 2 != chip, 0, jnp.where(kind == 3, 2, 1)) + jnp.where(stays, 0, 3)
    total = tiles.shape[0]
    quarter_count = total // 4
    index = jnp.arange(total, dtype=jnp.int32)
    key = bucket * total + index
    rank = jnp.sum((key[:, None] > key[None, :]).astype(jnp.int32), axis=1)
    placed = rank[None, :] == index[:, None]
    order = jnp.sum(jnp.where(placed, index[None, :], 0), axis=1)
    meta = jnp.sum(jnp.where(placed, meta[None, :], 0), axis=1)
    bound_keep = jnp.sum((bucket == 1).astype(jnp.int32), keepdims=True)
    bound_send = jnp.sum((bucket == 4).astype(jnp.int32), keepdims=True)
    padding = jnp.zeros((127,), jnp.int32)
    order, outbox = lax.optimization_barrier((order, outbox))
    send_cross, send_own = gather_tiles(
        order, tiles, 2 * quarter_count, 2, quarter_count, "pack_send"
    )
    recv_cross = permute(send_cross, beside)
    recv_own = permute(send_own, beside)
    meta_recv = permute(
        jnp.concatenate([meta[2 * quarter_count :], bound_send, padding]), beside
    )
    keep_cross, keep_own = gather_tiles(
        order, tiles, 0, 2, quarter_count, "pack_keep"
    )
    bounds = jnp.concatenate([bound_keep, meta_recv[2 * quarter_count : 2 * quarter_count + 1]])

    own_keep = meta[quarter_count : 2 * quarter_count]
    own_recv = meta_recv[quarter_count : 2 * quarter_count]
    cross_keep = meta[:quarter_count]
    cross_recv = meta_recv[:quarter_count]
    (
        other_chip,
        halo_early,
        inbox,
        keep_cross,
        keep_own,
        outbox,
        bounds,
        own_keep,
        own_recv,
        cross_keep,
        cross_recv,
        places,
    ) = lax.optimization_barrier(
        (
            other_chip,
            halo_early,
            inbox,
            keep_cross,
            keep_own,
            outbox,
            bounds,
            own_keep,
            own_recv,
            cross_keep,
            cross_recv,
            places,
        )
    )

    other_beside = permute(other_chip, beside)
    halo_late = permute(other_chip, late)
    early_beside = permute(halo_early, beside)
    inbox += [exchange(part) for part in outbox[1:]]
    group_pieces = (blocks, own_beside, other_chip, other_beside)
    cross = sums(
        bits,
        True,
        jnp.bfloat16,
        cross_keep,
        cross_recv,
        bounds,
        keep_cross,
        recv_cross,
        group_pieces + (halo_early, early_beside),
        "cross",
    )
    other_sums = permute(cross, across)
    early_sums = sums(
        bits,
        False,
        jnp.float32,
        own_keep,
        own_recv,
        bounds,
        keep_own,
        recv_own,
        group_pieces,
        "own",
    )
    halo_late, early_sums, inbox = lax.optimization_barrier((halo_late, early_sums, inbox))
    late_beside = permute(halo_late, beside)
    near = near_sums(
        bits,
        own_keep,
        own_recv,
        bounds,
        early_sums,
        other_sums,
        keep_own,
        recv_own,
        halo_late,
        late_beside,
    )
    result = apply_inverses(places, near, inbox)
    return near.reshape(own * size, columns), result.reshape(own * size, columns)


def solution(mesh):
    spec = P(AXES, None)
    spec3 = P(AXES, None, None)
    return jax.shard_map(
        functools.partial(per_device, mesh.shape["rows"], mesh.shape["cols"]),
        mesh=mesh,
        in_specs=(spec, spec3, spec, spec3, P()),
        out_specs=(spec, spec),
        check_vma=False,
    )
```

```python
import functools
import math

import jax
import jax.numpy as jnp
from jax import lax
from jax.experimental import pallas as pl
from jax.experimental.pallas import tpu as pltpu
from jax.sharding import PartitionSpec as P

AXES = ("rows", "cols")
MIB = 1024 * 1024
HBM = pl.BlockSpec(memory_space=pltpu.HBM)
SMEM = pl.BlockSpec(memory_space=pltpu.SMEM)
VMEM = pl.BlockSpec(memory_space=pltpu.VMEM)
CHUNK = 16


def params(mib):
    return pltpu.CompilerParams(vmem_limit_bytes=mib * MIB)


def cost(flops, mib):
    return pl.CostEstimate(flops=flops, bytes_accessed=mib * MIB, transcendentals=0)


def gather_kernel(first, order_ref, tiles, *rest):
    outs, (held, sem) = rest[:-2], rest[-2:]
    parts = len(outs)
    count = outs[0].shape[0]
    for part in range(parts):

        def fetch(turn, carry):
            place = part * count + turn
            pltpu.make_async_copy(
                tiles.at[order_ref[first + place]], held.at[place], sem.at[part]
            ).start()
            return carry

        lax.fori_loop(0, count, fetch, 0, unroll=4)
    copies = []
    for part, out in enumerate(outs):
        block = held.at[pl.ds(part * count, count)]
        pltpu.make_async_copy(block, block, sem.at[part]).wait()
        copies.append(pltpu.make_async_copy(block, out, sem.at[parts + part]))
        copies[-1].start()
    for copy in copies:
        copy.wait()


def gather_tiles(order, tiles, first, parts, count, name):
    block = (count,) + tiles.shape[1:]
    return pl.pallas_call(
        functools.partial(gather_kernel, first),
        out_shape=(jax.ShapeDtypeStruct(block, tiles.dtype),) * parts,
        in_specs=[SMEM, HBM],
        out_specs=(HBM,) * parts,
        scratch_shapes=[
            pltpu.VMEM((parts * count,) + tiles.shape[1:], tiles.dtype),
            pltpu.SemaphoreType.DMA((2 * parts,)),
        ],
        compiler_params=params(63),
        cost_estimate=pl.CostEstimate(
            flops=0, bytes_accessed=8 * parts * math.prod(block), transcendentals=0
        ),
        name=name,
    )(order, tiles)


def add_tiles(meta_ref, place, count, tiles, start, band, acc, bits):
    mask = (1 << bits) - 1
    for turn in range(count):
        meta = meta_ref[place + turn]
        row = lax.shift_right_logical(meta, bits)
        acc[row] += jnp.dot(
            tiles[start + turn], band[meta & mask], preferred_element_type=jnp.float32
        )


def sums_kernel(bits, whole, meta_keep, meta_recv, bounds, keep, recv, *rest):
    count = keep.shape[0]
    pieces, (out, band, mine, theirs, acc, sem) = rest[:-6], rest[-6:]
    size = pieces[0].shape[0]
    loads = [
        pltpu.make_async_copy(part, band.at[pl.ds(place * size, size)], sem.at[0])
        for place, part in enumerate(pieces)
    ]
    loads.append(pltpu.make_async_copy(keep, mine, sem.at[1]))
    loads.append(pltpu.make_async_copy(recv, theirs, sem.at[2]))
    for load in loads:
        load.start()
    acc[...] = jnp.zeros_like(acc)
    pltpu.make_async_copy(band, band, sem.at[0]).wait()
    for side, (meta, held) in enumerate(((meta_keep, mine), (meta_recv, theirs))):
        loads[len(pieces) + side].wait()
        if whole:

            def add(turn, carry):
                add_tiles(meta, turn * CHUNK, CHUNK, held, turn * CHUNK, band, acc, bits)
                return carry

            lax.fori_loop(0, count // CHUNK, add, 0)
        else:

            def add_one(turn, carry):
                add_tiles(meta, turn, 1, held, turn, band, acc, bits)
                return carry

            end = bounds[side]
            even = end // 8 * 8

            def add_eight(turn, carry):
                add_tiles(meta, turn * 8, 8, held, turn * 8, band, acc, bits)
                return carry

            lax.fori_loop(0, end // 8, add_eight, 0)
            lax.fori_loop(even, end, add_one, 0)
    out[...] = acc[...].astype(out.dtype)


def sums(bits, whole, dtype, meta_keep, meta_recv, bounds, keep, recv, pieces, name):
    block = pieces[0].shape
    held = pltpu.VMEM(keep.shape, keep.dtype)
    return pl.pallas_call(
        functools.partial(sums_kernel, bits, whole),
        out_shape=jax.ShapeDtypeStruct(block, dtype),
        in_specs=[SMEM] * 3 + [HBM] * (2 + len(pieces)),
        out_specs=VMEM,
        scratch_shapes=[
            pltpu.VMEM((len(pieces) * block[0],) + block[1:], jnp.bfloat16),
            held,
            held,
            pltpu.VMEM(block, jnp.float32),
            pltpu.SemaphoreType.DMA((3,)),
        ],
        compiler_params=params(63),
        cost_estimate=cost(4 * keep.size * block[2], 24),
        name=name,
    )(meta_keep, meta_recv, bounds, keep, recv, *pieces)


def near_kernel(bits, meta_keep, meta_recv, bounds, early, other, keep, recv, late, beside, *rest):
    near, acc, sent, band, mine, theirs, sem = rest
    count = keep.shape[0]
    size = late.shape[0]
    loads = [
        pltpu.make_async_copy(early, acc, sem.at[0]),
        pltpu.make_async_copy(late, band.at[pl.ds(0, size)], sem.at[2]),
        pltpu.make_async_copy(beside, band.at[pl.ds(size, size)], sem.at[3]),
        pltpu.make_async_copy(other, sent, sem.at[1]),
    ]
    for load in loads:
        load.start()
    sides = ((meta_keep, keep, mine), (meta_recv, recv, theirs))

    def chunk_copy(side, chunk):
        start = pl.multiple_of(chunk * CHUNK, CHUNK)
        piece = pl.ds(start, CHUNK)
        return pltpu.make_async_copy(
            sides[side][1].at[piece], sides[side][2].at[piece], sem.at[4 + side]
        )

    for side in (0, 1):

        def fetch(chunk, carry):
            chunk_copy(side, chunk).start()
            return carry

        lax.fori_loop(bounds[side] // CHUNK, count // CHUNK, fetch, 0)
    for side in (0, 1):

        def settle(chunk, carry):
            chunk_copy(side, chunk).wait()
            return carry

        lax.fori_loop(bounds[side] // CHUNK, count // CHUNK, settle, 0)
    for load in loads:
        load.wait()
    for side, (meta_ref, keep_ref, held) in enumerate(sides):

        def add(turn, carry):
            meta = meta_ref[turn]
            row = lax.shift_right_logical(meta, bits)
            slot = (meta & ((1 << bits) - 1)) - 4 * size
            acc[row] += jnp.dot(held[turn], band[slot], preferred_element_type=jnp.float32)
            return carry

        def add_eight(turn, carry):
            for step in range(8):
                add(turn * 8 + step, carry)
            return carry

        first = bounds[side]
        even = (first + 7) // 8
        lax.fori_loop(first, even * 8, add, 0)
        lax.fori_loop(even, count // 8, add_eight, 0)
    near[...] = (acc[...] + sent[...].astype(jnp.float32)).astype(jnp.bfloat16)


def near_sums(bits, meta_keep, meta_recv, bounds, early, other, keep, recv, late, beside):
    block = late.shape
    held = pltpu.VMEM(keep.shape, keep.dtype)
    return pl.pallas_call(
        functools.partial(near_kernel, bits),
        out_shape=jax.ShapeDtypeStruct(block, jnp.bfloat16),
        in_specs=[SMEM] * 3 + [HBM] * 6,
        out_specs=VMEM,
        scratch_shapes=[
            pltpu.VMEM(block, jnp.float32),
            pltpu.VMEM(block, jnp.bfloat16),
            pltpu.VMEM((2 * block[0],) + block[1:], jnp.bfloat16),
            held,
            held,
            pltpu.SemaphoreType.DMA((6,)),
        ],
        compiler_params=params(63),
        cost_estimate=cost(2 * keep.size * block[2], 18),
        name="near",
    )(meta_keep, meta_recv, bounds, early, other, keep, recv, late, beside)


def apply_kernel(places, near, *rest):
    inbox, (out, inverse, sem) = rest[:-3], rest[-3:]
    loads = []
    for place, part in enumerate(inbox):
        count = part.shape[0]
        loads.append(
            pltpu.make_async_copy(part, inverse.at[pl.ds(place * count, count)], sem.at[place])
        )
        loads[-1].start()
    for load in loads:
        load.wait()

    def apply(turn, carry):
        out[turn] = jnp.dot(
            inverse[places[turn]], near[turn], preferred_element_type=jnp.float32
        ).astype(jnp.bfloat16)
        return carry

    lax.fori_loop(0, near.shape[0], apply, 0, unroll=16)


def apply_inverses(places, near, inbox):
    block = inbox[0].shape
    return pl.pallas_call(
        apply_kernel,
        out_shape=jax.ShapeDtypeStruct(near.shape, jnp.bfloat16),
        in_specs=[SMEM, VMEM] + [HBM] * len(inbox),
        out_specs=VMEM,
        scratch_shapes=[
            pltpu.VMEM((len(inbox) * block[0],) + block[1:], jnp.bfloat16),
            pltpu.SemaphoreType.DMA((len(inbox),)),
        ],
        compiler_params=params(63),
        cost_estimate=cost(2 * near.size * near.shape[1], 6),
        name="apply",
    )(places, near, *inbox)


def ranks_by(labels, key):
    same = labels[:, None] == labels[None, :]
    return jnp.sum((same & (key[:, None] > key[None, :])).astype(jnp.int32), axis=1)


def pick(values, wanted):
    position = jnp.arange(values.shape[0], dtype=jnp.int32)
    hit = wanted[:, None] == values[None, :]
    return jnp.sum(jnp.where(hit, position[None, :], 0), axis=1)


def per_device(rows, cols, sources, tiles, block_list, inverses, slot_cluster):
    size = tiles.shape[1]
    columns = sources.shape[1]
    own = sources.shape[0] // size
    devices = rows * cols
    half = cols // 2
    row = lax.axis_index("rows")
    col = lax.axis_index("cols")
    chip, core = col // 2, col % 2
    myself = row * cols + col
    blocks = sources.reshape(own, size, columns)

    def number(r, x, c):
        return r * cols + x * 2 + c

    def permute(value, pairs):
        return lax.ppermute(value, AXES, pairs)

    lines = [(x, c) for x in range(half) for c in range(2)]
    across = [
        (number(r, x, c), number(r, 1 - x, c)) for r in range(rows) for x, c in lines
    ]
    beside = [
        (number(r, x, c), number(r, x, 1 - c)) for r in range(rows) for x, c in lines
    ]
    up = [(r, r + 1) for r in range(rows - 1)]
    down = [(b, a) for a, b in up]
    early = [
        (number(a, x, c), number(b, x, c))
        for x, c in lines
        for a, b in (down if x == 0 else up)
    ]
    late = [
        (number(a, x, c), number(b, x, c))
        for x, c in lines
        for a, b in (up if x == 0 else down)
    ]

    other_chip = permute(blocks, across)
    halo_early = permute(blocks, early)
    own_beside = permute(blocks, beside)

    capacity = -(-own // devices)
    local = jnp.arange(own, dtype=jnp.int32)
    source = pick(slot_cluster, myself * own + local) // own
    places = source * capacity + ranks_by(source, local)
    held = lax.dynamic_slice_in_dim(slot_cluster, myself * own, own, 0)
    target = held // own
    place_held = target * capacity + ranks_by(target, held % own)
    outbox_order = pick(place_held, jnp.arange(devices * capacity, dtype=jnp.int32))
    outbox = gather_tiles(outbox_order, inverses, 0, 1, devices * capacity, "pack_inverses")

    def exchange(value):
        return lax.all_to_all(value, AXES, split_axis=0, concat_axis=0, tiled=True)


    group = own * cols
    base = row * group
    bits = (8 * own - 1).bit_length()
    row_in = block_list[:, 0] - base
    owner = row_in // own
    column = block_list[:, 1] - base + group // 2
    quarter = column // own
    side = jnp.where(chip == 0, quarter // 2, 3 - quarter // 2)
    kind = (side + 3) % 4
    stays = owner % 2 == core
    reader = jnp.where(stays, core, 1 - core)
    slot = (jnp.minimum(kind, 2) * 2 + (quarter % 2 != reader)) * own + column % own
    meta = (row_in % own) * (1 << bits) + slot
    bucket = jnp.where(owner // 2 != chip, 0, jnp.where(kind == 3, 2, 1)) + jnp.where(stays, 0, 3)
    total = tiles.shape[0]
    quarter_count = total // 4
    index = jnp.arange(total, dtype=jnp.int32)
    key = bucket * total + index
    rank = jnp.sum((key[:, None] > key[None, :]).astype(jnp.int32), axis=1)
    placed = rank[None, :] == index[:, None]
    order = jnp.sum(jnp.where(placed, index[None, :], 0), axis=1)
    meta = jnp.sum(jnp.where(placed, meta[None, :], 0), axis=1)
    bound_keep = jnp.sum((bucket == 1).astype(jnp.int32), keepdims=True)
    bound_send = jnp.sum((bucket == 4).astype(jnp.int32), keepdims=True)
    padding = jnp.zeros((127,), jnp.int32)
    order, outbox = lax.optimization_barrier((order, outbox))
    send_cross, send_own = gather_tiles(
        order, tiles, 2 * quarter_count, 2, quarter_count, "pack_send"
    )
    recv_cross = permute(send_cross, beside)
    recv_own = permute(send_own, beside)
    meta_recv = permute(
        jnp.concatenate([meta[2 * quarter_count :], bound_send, padding]), beside
    )
    keep_cross, keep_own = gather_tiles(
        order, tiles, 0, 2, quarter_count, "pack_keep"
    )
    bounds = jnp.concatenate([bound_keep, meta_recv[2 * quarter_count : 2 * quarter_count + 1]])

    own_keep = meta[quarter_count : 2 * quarter_count]
    own_recv = meta_recv[quarter_count : 2 * quarter_count]
    cross_keep = meta[:quarter_count]
    cross_recv = meta_recv[:quarter_count]
    (
        other_chip,
        halo_early,
        keep_cross,
        keep_own,
        outbox,
        bounds,
        own_keep,
        own_recv,
        cross_keep,
        cross_recv,
        places,
    ) = lax.optimization_barrier(
        (
            other_chip,
            halo_early,
            keep_cross,
            keep_own,
            outbox,
            bounds,
            own_keep,
            own_recv,
            cross_keep,
            cross_recv,
            places,
        )
    )

    other_beside = permute(other_chip, beside)
    halo_late = permute(other_chip, late)
    early_beside = permute(halo_early, beside)
    inbox = [exchange(part) for part in outbox]
    group_pieces = (blocks, own_beside, other_chip, other_beside)
    cross = sums(
        bits,
        True,
        jnp.bfloat16,
        cross_keep,
        cross_recv,
        bounds,
        keep_cross,
        recv_cross,
        group_pieces + (halo_early, early_beside),
        "cross",
    )
    other_sums = permute(cross, across)
    early_sums = sums(
        bits,
        False,
        jnp.float32,
        own_keep,
        own_recv,
        bounds,
        keep_own,
        recv_own,
        group_pieces,
        "own",
    )
    halo_late, early_sums = lax.optimization_barrier((halo_late, early_sums))
    late_beside = permute(halo_late, beside)
    near = near_sums(
        bits,
        own_keep,
        own_recv,
        bounds,
        early_sums,
        other_sums,
        keep_own,
        recv_own,
        halo_late,
        late_beside,
    )
    result = apply_inverses(places, near, inbox)
    return near.reshape(own * size, columns), result.reshape(own * size, columns)


def solution(mesh):
    spec = P(AXES, None)
    spec3 = P(AXES, None, None)
    return jax.shard_map(
        functools.partial(per_device, mesh.shape["rows"], mesh.shape["cols"]),
        mesh=mesh,
        in_specs=(spec, spec3, spec, spec3, P()),
        out_specs=(spec, spec),
        check_vma=False,
    )
```

```python
import functools
import math

import jax
import jax.numpy as jnp
from jax import lax
from jax.experimental import pallas as pl
from jax.experimental.pallas import tpu as pltpu
from jax.sharding import PartitionSpec as P

AXES = ("rows", "cols")
MIB = 1024 * 1024
HBM = pl.BlockSpec(memory_space=pltpu.HBM)
SMEM = pl.BlockSpec(memory_space=pltpu.SMEM)
VMEM = pl.BlockSpec(memory_space=pltpu.VMEM)
CHUNK = 16


def params(mib):
    return pltpu.CompilerParams(vmem_limit_bytes=mib * MIB)


def cost(flops, mib):
    return pl.CostEstimate(flops=flops, bytes_accessed=mib * MIB, transcendentals=0)


def gather_kernel(first, order_ref, tiles, *rest):
    outs, (held, sem) = rest[:-2], rest[-2:]
    parts = len(outs)
    count = outs[0].shape[0]
    for part in range(parts):

        def fetch(turn, carry):
            place = part * count + turn
            pltpu.make_async_copy(
                tiles.at[order_ref[first + place]], held.at[place], sem.at[part]
            ).start()
            return carry

        lax.fori_loop(0, count, fetch, 0, unroll=4)
    copies = []
    for part, out in enumerate(outs):
        block = held.at[pl.ds(part * count, count)]
        pltpu.make_async_copy(block, block, sem.at[part]).wait()
        copies.append(pltpu.make_async_copy(block, out, sem.at[parts + part]))
        copies[-1].start()
    for copy in copies:
        copy.wait()


def gather_tiles(order, tiles, first, parts, count, name):
    block = (count,) + tiles.shape[1:]
    return pl.pallas_call(
        functools.partial(gather_kernel, first),
        out_shape=(jax.ShapeDtypeStruct(block, tiles.dtype),) * parts,
        in_specs=[SMEM, HBM],
        out_specs=(HBM,) * parts,
        scratch_shapes=[
            pltpu.VMEM((parts * count,) + tiles.shape[1:], tiles.dtype),
            pltpu.SemaphoreType.DMA((2 * parts,)),
        ],
        compiler_params=params(63),
        cost_estimate=pl.CostEstimate(
            flops=0, bytes_accessed=8 * parts * math.prod(block), transcendentals=0
        ),
        name=name,
    )(order, tiles)


def add_tiles(meta_ref, place, count, tiles, start, band, acc, bits):
    mask = (1 << bits) - 1
    for turn in range(count):
        meta = meta_ref[place + turn]
        row = lax.shift_right_logical(meta, bits)
        acc[row] += jnp.dot(
            tiles[start + turn], band[meta & mask], preferred_element_type=jnp.float32
        )


def sums_kernel(bits, whole, meta_keep, meta_recv, bounds, keep, recv, *rest):
    count = keep.shape[0]
    pieces, (out, band, mine, theirs, acc, sem) = rest[:-6], rest[-6:]
    size = pieces[0].shape[0]
    loads = [
        pltpu.make_async_copy(part, band.at[pl.ds(place * size, size)], sem.at[0])
        for place, part in enumerate(pieces)
    ]
    loads.append(pltpu.make_async_copy(keep, mine, sem.at[1]))
    loads.append(pltpu.make_async_copy(recv, theirs, sem.at[2]))
    for load in loads:
        load.start()
    acc[...] = jnp.zeros_like(acc)
    pltpu.make_async_copy(band, band, sem.at[0]).wait()
    for side, (meta, held) in enumerate(((meta_keep, mine), (meta_recv, theirs))):
        loads[len(pieces) + side].wait()
        if whole:

            def add(turn, carry):
                add_tiles(meta, turn * CHUNK, CHUNK, held, turn * CHUNK, band, acc, bits)
                return carry

            lax.fori_loop(0, count // CHUNK, add, 0)
        else:

            def add_one(turn, carry):
                add_tiles(meta, turn, 1, held, turn, band, acc, bits)
                return carry

            end = bounds[side]
            even = end // 8 * 8

            def add_eight(turn, carry):
                add_tiles(meta, turn * 8, 8, held, turn * 8, band, acc, bits)
                return carry

            lax.fori_loop(0, end // 8, add_eight, 0)
            lax.fori_loop(even, end, add_one, 0)
    out[...] = acc[...].astype(out.dtype)


def sums(bits, whole, dtype, meta_keep, meta_recv, bounds, keep, recv, pieces, name):
    block = pieces[0].shape
    held = pltpu.VMEM(keep.shape, keep.dtype)
    return pl.pallas_call(
        functools.partial(sums_kernel, bits, whole),
        out_shape=jax.ShapeDtypeStruct(block, dtype),
        in_specs=[SMEM] * 3 + [HBM] * (2 + len(pieces)),
        out_specs=VMEM,
        scratch_shapes=[
            pltpu.VMEM((len(pieces) * block[0],) + block[1:], jnp.bfloat16),
            held,
            held,
            pltpu.VMEM(block, jnp.float32),
            pltpu.SemaphoreType.DMA((3,)),
        ],
        compiler_params=params(63),
        cost_estimate=cost(4 * keep.size * block[2], 24),
        name=name,
    )(meta_keep, meta_recv, bounds, keep, recv, *pieces)


def near_kernel(bits, meta_keep, meta_recv, bounds, early, other, keep, recv, *rest):
    pieces, (near, acc, sent, band, mine, theirs, sem) = rest[:-7], rest[-7:]
    count = keep.shape[0]
    size = acc.shape[0]
    loads = [
        pltpu.make_async_copy(early, acc, sem.at[0]),
        pltpu.make_async_copy(other, sent, sem.at[1]),
    ]
    place = 0
    for order, piece in enumerate(pieces):
        part = band.at[pl.ds(place, piece.shape[0])]
        loads.append(pltpu.make_async_copy(piece, part, sem.at[4 + order]))
        place += piece.shape[0]
    for load in loads:
        load.start()
    sides = ((meta_keep, keep, mine), (meta_recv, recv, theirs))

    def chunk_copy(side, chunk):
        start = pl.multiple_of(chunk * CHUNK, CHUNK)
        piece = pl.ds(start, CHUNK)
        return pltpu.make_async_copy(
            sides[side][1].at[piece], sides[side][2].at[piece], sem.at[2 + side]
        )

    for side in (0, 1):

        def fetch(chunk, carry):
            chunk_copy(side, chunk).start()
            return carry

        lax.fori_loop(bounds[side] // CHUNK, count // CHUNK, fetch, 0)
    for side in (0, 1):

        def settle(chunk, carry):
            chunk_copy(side, chunk).wait()
            return carry

        lax.fori_loop(bounds[side] // CHUNK, count // CHUNK, settle, 0)
    for load in loads:
        load.wait()
    for side, (meta_ref, keep_ref, held) in enumerate(sides):

        def add(turn, carry):
            meta = meta_ref[turn]
            row = lax.shift_right_logical(meta, bits)
            slot = (meta & ((1 << bits) - 1)) - 4 * size
            acc[row] += jnp.dot(held[turn], band[slot], preferred_element_type=jnp.float32)
            return carry

        def add_eight(turn, carry):
            for step in range(8):
                add(turn * 8 + step, carry)
            return carry

        first = bounds[side]
        even = (first + 7) // 8
        lax.fori_loop(first, even * 8, add, 0)
        lax.fori_loop(even, count // 8, add_eight, 0)
    near[...] = (acc[...] + sent[...].astype(jnp.float32)).astype(jnp.bfloat16)


def near_sums(bits, meta_keep, meta_recv, bounds, early, other, keep, recv, pieces):
    block = early.shape
    held = pltpu.VMEM(keep.shape, keep.dtype)
    return pl.pallas_call(
        functools.partial(near_kernel, bits),
        out_shape=jax.ShapeDtypeStruct(block, jnp.bfloat16),
        in_specs=[SMEM] * 3 + [HBM] * (4 + len(pieces)),
        out_specs=VMEM,
        scratch_shapes=[
            pltpu.VMEM(block, jnp.float32),
            pltpu.VMEM(block, jnp.bfloat16),
            pltpu.VMEM((2 * block[0],) + block[1:], jnp.bfloat16),
            held,
            held,
            pltpu.SemaphoreType.DMA((4 + len(pieces),)),
        ],
        compiler_params=params(63),
        cost_estimate=cost(2 * keep.size * block[2], 18),
        name="near",
    )(meta_keep, meta_recv, bounds, early, other, keep, recv, *pieces)


def apply_kernel(places, near, *rest):
    inbox, (out, inverse, sem) = rest[:-3], rest[-3:]
    loads = []
    for place, part in enumerate(inbox):
        count = part.shape[0]
        loads.append(
            pltpu.make_async_copy(part, inverse.at[pl.ds(place * count, count)], sem.at[place])
        )
        loads[-1].start()
    for load in loads:
        load.wait()

    def apply(turn, carry):
        out[turn] = jnp.dot(
            inverse[places[turn]], near[turn], preferred_element_type=jnp.float32
        ).astype(jnp.bfloat16)
        return carry

    lax.fori_loop(0, near.shape[0], apply, 0, unroll=16)


def apply_inverses(places, near, inbox):
    block = inbox[0].shape
    return pl.pallas_call(
        apply_kernel,
        out_shape=jax.ShapeDtypeStruct(near.shape, jnp.bfloat16),
        in_specs=[SMEM, VMEM] + [HBM] * len(inbox),
        out_specs=VMEM,
        scratch_shapes=[
            pltpu.VMEM((len(inbox) * block[0],) + block[1:], jnp.bfloat16),
            pltpu.SemaphoreType.DMA((len(inbox),)),
        ],
        compiler_params=params(63),
        cost_estimate=cost(2 * near.size * near.shape[1], 6),
        name="apply",
    )(places, near, *inbox)


def ranks_by(labels, key):
    same = labels[:, None] == labels[None, :]
    return jnp.sum((same & (key[:, None] > key[None, :])).astype(jnp.int32), axis=1)


def pick(values, wanted):
    position = jnp.arange(values.shape[0], dtype=jnp.int32)
    hit = wanted[:, None] == values[None, :]
    return jnp.sum(jnp.where(hit, position[None, :], 0), axis=1)


def per_device(rows, cols, sources, tiles, block_list, inverses, slot_cluster):
    size = tiles.shape[1]
    columns = sources.shape[1]
    own = sources.shape[0] // size
    devices = rows * cols
    half = cols // 2
    row = lax.axis_index("rows")
    col = lax.axis_index("cols")
    chip, core = col // 2, col % 2
    myself = row * cols + col
    blocks = sources.reshape(own, size, columns)

    def number(r, x, c):
        return r * cols + x * 2 + c

    def permute(value, pairs):
        return lax.ppermute(value, AXES, pairs)

    lines = [(x, c) for x in range(half) for c in range(2)]
    across = [
        (number(r, x, c), number(r, 1 - x, c)) for r in range(rows) for x, c in lines
    ]
    beside = [
        (number(r, x, c), number(r, x, 1 - c)) for r in range(rows) for x, c in lines
    ]
    up = [(r, r + 1) for r in range(rows - 1)]
    down = [(b, a) for a, b in up]
    early = [
        (number(a, x, c), number(b, x, c))
        for x, c in lines
        for a, b in (down if x == 0 else up)
    ]
    late = [
        (number(a, x, c), number(b, x, c))
        for x, c in lines
        for a, b in (up if x == 0 else down)
    ]

    other_chip = permute(blocks, across)
    halo_early = permute(blocks, early)
    own_beside = permute(blocks, beside)

    capacity = -(-own // devices)
    local = jnp.arange(own, dtype=jnp.int32)
    source = pick(slot_cluster, myself * own + local) // own
    places = source * capacity + ranks_by(source, local)
    held = lax.dynamic_slice_in_dim(slot_cluster, myself * own, own, 0)
    target = held // own
    place_held = target * capacity + ranks_by(target, held % own)
    outbox_order = pick(place_held, jnp.arange(devices * capacity, dtype=jnp.int32))
    outbox = gather_tiles(outbox_order, inverses, 0, 1, devices * capacity, "pack_inverses")

    def exchange(value):
        return lax.all_to_all(value, AXES, split_axis=0, concat_axis=0, tiled=True)


    group = own * cols
    base = row * group
    bits = (8 * own - 1).bit_length()
    row_in = block_list[:, 0] - base
    owner = row_in // own
    column = block_list[:, 1] - base + group // 2
    quarter = column // own
    side = jnp.where(chip == 0, quarter // 2, 3 - quarter // 2)
    kind = (side + 3) % 4
    stays = owner % 2 == core
    reader = jnp.where(stays, core, 1 - core)
    slot = (jnp.minimum(kind, 2) * 2 + (quarter % 2 != reader)) * own + column % own
    meta = (row_in % own) * (1 << bits) + slot
    bucket = jnp.where(owner // 2 != chip, 0, jnp.where(kind == 3, 2, 1)) + jnp.where(stays, 0, 3)
    total = tiles.shape[0]
    quarter_count = total // 4
    index = jnp.arange(total, dtype=jnp.int32)
    key = bucket * total + index
    rank = jnp.sum((key[:, None] > key[None, :]).astype(jnp.int32), axis=1)
    placed = rank[None, :] == index[:, None]
    order = jnp.sum(jnp.where(placed, index[None, :], 0), axis=1)
    meta = jnp.sum(jnp.where(placed, meta[None, :], 0), axis=1)
    bound_keep = jnp.sum((bucket == 1).astype(jnp.int32), keepdims=True)
    bound_send = jnp.sum((bucket == 4).astype(jnp.int32), keepdims=True)
    padding = jnp.zeros((127,), jnp.int32)
    order, outbox = lax.optimization_barrier((order, outbox))
    send_cross, send_own = gather_tiles(
        order, tiles, 2 * quarter_count, 2, quarter_count, "pack_send"
    )
    recv_cross = permute(send_cross, beside)
    recv_own = permute(send_own, beside)
    meta_recv = permute(
        jnp.concatenate([meta[2 * quarter_count :], bound_send, padding]), beside
    )
    keep_cross, keep_own = gather_tiles(
        order, tiles, 0, 2, quarter_count, "pack_keep"
    )
    bounds = jnp.concatenate([bound_keep, meta_recv[2 * quarter_count : 2 * quarter_count + 1]])

    own_keep = meta[quarter_count : 2 * quarter_count]
    own_recv = meta_recv[quarter_count : 2 * quarter_count]
    cross_keep = meta[:quarter_count]
    cross_recv = meta_recv[:quarter_count]
    (
        other_chip,
        halo_early,
        keep_cross,
        keep_own,
        outbox,
        bounds,
        own_keep,
        own_recv,
        cross_keep,
        cross_recv,
        places,
    ) = lax.optimization_barrier(
        (
            other_chip,
            halo_early,
            keep_cross,
            keep_own,
            outbox,
            bounds,
            own_keep,
            own_recv,
            cross_keep,
            cross_recv,
            places,
        )
    )

    other_beside = permute(other_chip, beside)
    cut = own - own // 4
    halo_late = permute(other_chip[:cut], late)
    halo_across = permute(halo_early[cut:], across)
    early_beside = permute(halo_early, beside)
    inbox = [exchange(part) for part in outbox]
    group_pieces = (blocks, own_beside, other_chip, other_beside)
    cross = sums(
        bits,
        True,
        jnp.bfloat16,
        cross_keep,
        cross_recv,
        bounds,
        keep_cross,
        recv_cross,
        group_pieces + (halo_early, early_beside),
        "cross",
    )
    other_sums = permute(cross, across)
    own_keep, halo_across = lax.optimization_barrier((own_keep, halo_across))
    early_sums = sums(
        bits,
        False,
        jnp.float32,
        own_keep,
        own_recv,
        bounds,
        keep_own,
        recv_own,
        group_pieces,
        "own",
    )
    halo_late, early_sums = lax.optimization_barrier((halo_late, early_sums))
    late_beside = permute(halo_late, beside)
    across_beside = permute(halo_across, beside)
    near = near_sums(
        bits,
        own_keep,
        own_recv,
        bounds,
        early_sums,
        other_sums,
        keep_own,
        recv_own,
        (halo_late, halo_across, late_beside, across_beside),
    )
    result = apply_inverses(places, near, inbox)
    return near.reshape(own * size, columns), result.reshape(own * size, columns)


def solution(mesh):
    spec = P(AXES, None)
    spec3 = P(AXES, None, None)
    return jax.shard_map(
        functools.partial(per_device, mesh.shape["rows"], mesh.shape["cols"]),
        mesh=mesh,
        in_specs=(spec, spec3, spec, spec3, P()),
        out_specs=(spec, spec),
        check_vma=False,
    )
```

```python
import functools
import math

import jax
import jax.numpy as jnp
from jax import lax
from jax.experimental import pallas as pl
from jax.experimental.pallas import tpu as pltpu
from jax.sharding import PartitionSpec as P

AXES = ("rows", "cols")
MIB = 1024 * 1024
HBM = pl.BlockSpec(memory_space=pltpu.HBM)
SMEM = pl.BlockSpec(memory_space=pltpu.SMEM)
VMEM = pl.BlockSpec(memory_space=pltpu.VMEM)
CHUNK = 16


def params(mib):
    return pltpu.CompilerParams(vmem_limit_bytes=mib * MIB)


def cost(flops, mib):
    return pl.CostEstimate(flops=flops, bytes_accessed=mib * MIB, transcendentals=0)


def gather_kernel(first, order_ref, tiles, *rest):
    outs, (held, sem) = rest[:-2], rest[-2:]
    parts = len(outs)
    count = outs[0].shape[0]
    for part in range(parts):

        def fetch(turn, carry):
            place = part * count + turn
            pltpu.make_async_copy(
                tiles.at[order_ref[first + place]], held.at[place], sem.at[part]
            ).start()
            return carry

        lax.fori_loop(0, count, fetch, 0, unroll=4)
    copies = []
    for part, out in enumerate(outs):
        block = held.at[pl.ds(part * count, count)]
        pltpu.make_async_copy(block, block, sem.at[part]).wait()
        copies.append(pltpu.make_async_copy(block, out, sem.at[parts + part]))
        copies[-1].start()
    for copy in copies:
        copy.wait()


def gather_tiles(order, tiles, first, parts, count, name):
    block = (count,) + tiles.shape[1:]
    return pl.pallas_call(
        functools.partial(gather_kernel, first),
        out_shape=(jax.ShapeDtypeStruct(block, tiles.dtype),) * parts,
        in_specs=[SMEM, HBM],
        out_specs=(HBM,) * parts,
        scratch_shapes=[
            pltpu.VMEM((parts * count,) + tiles.shape[1:], tiles.dtype),
            pltpu.SemaphoreType.DMA((2 * parts,)),
        ],
        compiler_params=params(63),
        cost_estimate=pl.CostEstimate(
            flops=0, bytes_accessed=8 * parts * math.prod(block), transcendentals=0
        ),
        name=name,
    )(order, tiles)


def split_kernel(cut, first, second, head, tail, held, sem):
    rest = held.shape[0] - cut
    parts = (
        (first.at[pl.ds(0, cut)], held.at[pl.ds(0, cut)], head),
        (second.at[pl.ds(cut, rest)], held.at[pl.ds(cut, rest)], tail),
    )
    loads = [pltpu.make_async_copy(a, b, sem.at[i]) for i, (a, b, c) in enumerate(parts)]
    stores = [pltpu.make_async_copy(b, c, sem.at[2 + i]) for i, (a, b, c) in enumerate(parts)]
    for load in loads:
        load.start()
    for load, store in zip(loads, stores):
        load.wait()
        store.start()
    for store in stores:
        store.wait()


def split(cut, first, second):
    tile = first.shape[1:]
    return pl.pallas_call(
        functools.partial(split_kernel, cut),
        out_shape=(
            jax.ShapeDtypeStruct((cut,) + tile, first.dtype),
            jax.ShapeDtypeStruct((first.shape[0] - cut,) + tile, first.dtype),
        ),
        in_specs=[HBM, HBM],
        out_specs=(HBM, HBM),
        scratch_shapes=[pltpu.VMEM(first.shape, first.dtype), pltpu.SemaphoreType.DMA((4,))],
        compiler_params=params(63),
        cost_estimate=cost(0, 4),
        name="split",
    )(first, second)


def add_tiles(meta_ref, place, count, tiles, start, band, acc, bits):
    mask = (1 << bits) - 1
    for turn in range(count):
        meta = meta_ref[place + turn]
        row = lax.shift_right_logical(meta, bits)
        acc[row] += jnp.dot(
            tiles[start + turn], band[meta & mask], preferred_element_type=jnp.float32
        )


def sums_kernel(bits, whole, meta_keep, meta_recv, bounds, keep, recv, *rest):
    count = keep.shape[0]
    pieces, (out, band, mine, theirs, acc, sem) = rest[:-6], rest[-6:]
    size = pieces[0].shape[0]
    loads = [
        pltpu.make_async_copy(part, band.at[pl.ds(place * size, size)], sem.at[0])
        for place, part in enumerate(pieces)
    ]
    loads.append(pltpu.make_async_copy(keep, mine, sem.at[1]))
    loads.append(pltpu.make_async_copy(recv, theirs, sem.at[2]))
    for load in loads:
        load.start()
    acc[...] = jnp.zeros_like(acc)
    pltpu.make_async_copy(band, band, sem.at[0]).wait()
    for side, (meta, held) in enumerate(((meta_keep, mine), (meta_recv, theirs))):
        loads[len(pieces) + side].wait()
        if whole:

            def add(turn, carry):
                add_tiles(meta, turn * CHUNK, CHUNK, held, turn * CHUNK, band, acc, bits)
                return carry

            lax.fori_loop(0, count // CHUNK, add, 0)
        else:

            def add_one(turn, carry):
                add_tiles(meta, turn, 1, held, turn, band, acc, bits)
                return carry

            end = bounds[side]
            even = end // 8 * 8

            def add_eight(turn, carry):
                add_tiles(meta, turn * 8, 8, held, turn * 8, band, acc, bits)
                return carry

            lax.fori_loop(0, end // 8, add_eight, 0)
            lax.fori_loop(even, end, add_one, 0)
    out[...] = acc[...].astype(out.dtype)


def sums(bits, whole, dtype, meta_keep, meta_recv, bounds, keep, recv, pieces, name):
    block = pieces[0].shape
    held = pltpu.VMEM(keep.shape, keep.dtype)
    return pl.pallas_call(
        functools.partial(sums_kernel, bits, whole),
        out_shape=jax.ShapeDtypeStruct(block, dtype),
        in_specs=[SMEM] * 3 + [HBM] * (2 + len(pieces)),
        out_specs=VMEM,
        scratch_shapes=[
            pltpu.VMEM((len(pieces) * block[0],) + block[1:], jnp.bfloat16),
            held,
            held,
            pltpu.VMEM(block, jnp.float32),
            pltpu.SemaphoreType.DMA((3,)),
        ],
        compiler_params=params(63),
        cost_estimate=cost(4 * keep.size * block[2], 24),
        name=name,
    )(meta_keep, meta_recv, bounds, keep, recv, *pieces)


def final_kernel(
    bits, meta_keep, meta_recv, bounds, places, early, other, keep, recv, inbox, *rest
):
    pieces, (near, out, acc, sent, band, mine, theirs, inverse, sem) = rest[:-9], rest[-9:]
    count = keep.shape[0]
    size = acc.shape[0]
    loads = [
        pltpu.make_async_copy(early, acc, sem.at[0]),
        pltpu.make_async_copy(other, sent, sem.at[1]),
    ]
    place = 0
    for order, piece in enumerate(pieces):
        part = band.at[pl.ds(place, piece.shape[0])]
        loads.append(pltpu.make_async_copy(piece, part, sem.at[4 + order]))
        place += piece.shape[0]
    for load in loads:
        load.start()
    inverses = pltpu.make_async_copy(inbox, inverse, sem.at[4 + len(pieces)])
    sides = ((meta_keep, keep, mine), (meta_recv, recv, theirs))

    def chunk_copy(side, chunk):
        start = pl.multiple_of(chunk * CHUNK, CHUNK)
        piece = pl.ds(start, CHUNK)
        return pltpu.make_async_copy(
            sides[side][1].at[piece], sides[side][2].at[piece], sem.at[2 + side]
        )

    for side in (0, 1):

        def fetch(chunk, carry):
            chunk_copy(side, chunk).start()
            return carry

        lax.fori_loop(bounds[side] // CHUNK, count // CHUNK, fetch, 0)
    inverses.start()
    for side in (0, 1):

        def settle(chunk, carry):
            chunk_copy(side, chunk).wait()
            return carry

        lax.fori_loop(bounds[side] // CHUNK, count // CHUNK, settle, 0)
    for load in loads:
        load.wait()
    for side, (meta_ref, keep_ref, held) in enumerate(sides):

        def add(turn, carry):
            meta = meta_ref[turn]
            row = lax.shift_right_logical(meta, bits)
            slot = (meta & ((1 << bits) - 1)) - 4 * size
            acc[row] += jnp.dot(held[turn], band[slot], preferred_element_type=jnp.float32)
            return carry

        def add_eight(turn, carry):
            for step in range(8):
                add(turn * 8 + step, carry)
            return carry

        first = bounds[side]
        even = (first + 7) // 8
        lax.fori_loop(first, even * 8, add, 0)
        lax.fori_loop(even, count // 8, add_eight, 0)
    inverses.wait()

    def apply(turn, carry):
        block = (acc[turn] + sent[turn].astype(jnp.float32)).astype(jnp.bfloat16)
        near[turn] = block
        out[turn] = jnp.dot(
            inverse[places[turn]], block, preferred_element_type=jnp.float32
        ).astype(jnp.bfloat16)
        return carry

    lax.fori_loop(0, size, apply, 0, unroll=16)


def final(
    bits, meta_keep, meta_recv, bounds, places, early, other, keep, recv, inbox, pieces
):
    block = early.shape
    held = pltpu.VMEM(keep.shape, keep.dtype)
    return pl.pallas_call(
        functools.partial(final_kernel, bits),
        out_shape=(jax.ShapeDtypeStruct(block, jnp.bfloat16),) * 2,
        in_specs=[SMEM] * 4 + [HBM] * (5 + len(pieces)),
        out_specs=(VMEM, VMEM),
        scratch_shapes=[
            pltpu.VMEM(block, jnp.float32),
            pltpu.VMEM(block, jnp.bfloat16),
            pltpu.VMEM((2 * block[0],) + block[1:], jnp.bfloat16),
            held,
            held,
            pltpu.VMEM(inbox.shape, jnp.bfloat16),
            pltpu.SemaphoreType.DMA((5 + len(pieces),)),
        ],
        compiler_params=params(63),
        cost_estimate=cost(3 * keep.size * block[2], 22),
        name="final",
    )(meta_keep, meta_recv, bounds, places, early, other, keep, recv, inbox, *pieces)


def ranks_by(labels, key):
    same = labels[:, None] == labels[None, :]
    return jnp.sum((same & (key[:, None] > key[None, :])).astype(jnp.int32), axis=1)


def pick(values, wanted):
    position = jnp.arange(values.shape[0], dtype=jnp.int32)
    hit = wanted[:, None] == values[None, :]
    return jnp.sum(jnp.where(hit, position[None, :], 0), axis=1)


def per_device(rows, cols, sources, tiles, block_list, inverses, slot_cluster):
    size = tiles.shape[1]
    columns = sources.shape[1]
    own = sources.shape[0] // size
    devices = rows * cols
    half = cols // 2
    row = lax.axis_index("rows")
    col = lax.axis_index("cols")
    chip, core = col // 2, col % 2
    myself = row * cols + col
    blocks = sources.reshape(own, size, columns)

    def number(r, x, c):
        return r * cols + x * 2 + c

    def permute(value, pairs):
        return lax.ppermute(value, AXES, pairs)

    lines = [(x, c) for x in range(half) for c in range(2)]
    across = [
        (number(r, x, c), number(r, 1 - x, c)) for r in range(rows) for x, c in lines
    ]
    beside = [
        (number(r, x, c), number(r, x, 1 - c)) for r in range(rows) for x, c in lines
    ]
    up = [(r, r + 1) for r in range(rows - 1)]
    down = [(b, a) for a, b in up]
    early = [
        (number(a, x, c), number(b, x, c))
        for x, c in lines
        for a, b in (down if x == 0 else up)
    ]
    late = [
        (number(a, x, c), number(b, x, c))
        for x, c in lines
        for a, b in (up if x == 0 else down)
    ]

    other_chip = permute(blocks, across)
    halo_early = permute(blocks, early)
    own_beside = permute(blocks, beside)

    capacity = -(-own // devices)
    local = jnp.arange(own, dtype=jnp.int32)
    source = pick(slot_cluster, myself * own + local) // own
    places = source * capacity + ranks_by(source, local)
    held = lax.dynamic_slice_in_dim(slot_cluster, myself * own, own, 0)
    target = held // own
    place_held = target * capacity + ranks_by(target, held % own)
    outbox_order = pick(place_held, jnp.arange(devices * capacity, dtype=jnp.int32))
    (outbox,) = gather_tiles(outbox_order, inverses, 0, 1, devices * capacity, "pack_inverses")

    def exchange(value):
        return lax.all_to_all(value, AXES, split_axis=0, concat_axis=0, tiled=True)


    group = own * cols
    base = row * group
    bits = (8 * own - 1).bit_length()
    row_in = block_list[:, 0] - base
    owner = row_in // own
    column = block_list[:, 1] - base + group // 2
    quarter = column // own
    side = jnp.where(chip == 0, quarter // 2, 3 - quarter // 2)
    kind = (side + 3) % 4
    stays = owner % 2 == core
    reader = jnp.where(stays, core, 1 - core)
    slot = (jnp.minimum(kind, 2) * 2 + (quarter % 2 != reader)) * own + column % own
    meta = (row_in % own) * (1 << bits) + slot
    bucket = jnp.where(owner // 2 != chip, 0, jnp.where(kind == 3, 2, 1)) + jnp.where(stays, 0, 3)
    total = tiles.shape[0]
    quarter_count = total // 4
    index = jnp.arange(total, dtype=jnp.int32)
    key = bucket * total + index
    rank = jnp.sum((key[:, None] > key[None, :]).astype(jnp.int32), axis=1)
    placed = rank[None, :] == index[:, None]
    order = jnp.sum(jnp.where(placed, index[None, :], 0), axis=1)
    meta = jnp.sum(jnp.where(placed, meta[None, :], 0), axis=1)
    bound_keep = jnp.sum((bucket == 1).astype(jnp.int32), keepdims=True)
    bound_send = jnp.sum((bucket == 4).astype(jnp.int32), keepdims=True)
    padding = jnp.zeros((127,), jnp.int32)
    order, outbox = lax.optimization_barrier((order, outbox))
    send_cross, send_own = gather_tiles(
        order, tiles, 2 * quarter_count, 2, quarter_count, "pack_send"
    )
    recv_cross = permute(send_cross, beside)
    recv_own = permute(send_own, beside)
    meta_recv = permute(
        jnp.concatenate([meta[2 * quarter_count :], bound_send, padding]), beside
    )
    keep_cross, keep_own = gather_tiles(
        order, tiles, 0, 2, quarter_count, "pack_keep"
    )
    bounds = jnp.concatenate([bound_keep, meta_recv[2 * quarter_count : 2 * quarter_count + 1]])

    own_keep = meta[quarter_count : 2 * quarter_count]
    own_recv = meta_recv[quarter_count : 2 * quarter_count]
    cross_keep = meta[:quarter_count]
    cross_recv = meta_recv[:quarter_count]
    (
        other_chip,
        halo_early,
        keep_cross,
        keep_own,
        outbox,
        bounds,
        own_keep,
        own_recv,
        cross_keep,
        cross_recv,
        places,
    ) = lax.optimization_barrier(
        (
            other_chip,
            halo_early,
            keep_cross,
            keep_own,
            outbox,
            bounds,
            own_keep,
            own_recv,
            cross_keep,
            cross_recv,
            places,
        )
    )

    other_beside = permute(other_chip, beside)
    cut = own - own // 4
    late_part, across_part = split(cut, other_chip, halo_early)
    halo_late = permute(late_part, late)
    halo_across = permute(across_part, across)
    inbox = exchange(outbox)
    early_beside = permute(halo_early, beside)
    group_pieces = (blocks, own_beside, other_chip, other_beside)
    cross = sums(
        bits,
        True,
        jnp.bfloat16,
        cross_keep,
        cross_recv,
        bounds,
        keep_cross,
        recv_cross,
        group_pieces + (halo_early, early_beside),
        "cross",
    )
    other_sums = permute(cross, across)
    own_keep, halo_across = lax.optimization_barrier((own_keep, halo_across))
    early_sums = sums(
        bits,
        False,
        jnp.float32,
        own_keep,
        own_recv,
        bounds,
        keep_own,
        recv_own,
        group_pieces,
        "own",
    )
    halo_late, early_sums = lax.optimization_barrier((halo_late, early_sums))
    late_beside = permute(halo_late, beside)
    across_beside = permute(halo_across, beside)
    near, result = final(
        bits,
        own_keep,
        own_recv,
        bounds,
        places,
        early_sums,
        other_sums,
        keep_own,
        recv_own,
        inbox,
        (halo_late, halo_across, late_beside, across_beside),
    )
    return near.reshape(own * size, columns), result.reshape(own * size, columns)


def solution(mesh):
    spec = P(AXES, None)
    spec3 = P(AXES, None, None)
    return jax.shard_map(
        functools.partial(per_device, mesh.shape["rows"], mesh.shape["cols"]),
        mesh=mesh,
        in_specs=(spec, spec3, spec, spec3, P()),
        out_specs=(spec, spec),
        check_vma=False,
    )
```

```python
import functools
import math

import jax
import jax.numpy as jnp
from jax import lax
from jax.experimental import pallas as pl
from jax.experimental.pallas import tpu as pltpu
from jax.sharding import PartitionSpec as P

AXES = ("rows", "cols")
MIB = 1024 * 1024
HBM = pl.BlockSpec(memory_space=pltpu.HBM)
SMEM = pl.BlockSpec(memory_space=pltpu.SMEM)
VMEM = pl.BlockSpec(memory_space=pltpu.VMEM)
CHUNK = 16


def params(mib):
    return pltpu.CompilerParams(vmem_limit_bytes=mib * MIB)


def cost(flops, mib):
    return pl.CostEstimate(flops=flops, bytes_accessed=mib * MIB, transcendentals=0)


def gather_kernel(first, order_ref, tiles, *rest):
    outs, (held, sem) = rest[:-2], rest[-2:]
    parts = len(outs)
    count = outs[0].shape[0]
    for part in range(parts):

        def fetch(turn, carry):
            place = part * count + turn
            pltpu.make_async_copy(
                tiles.at[order_ref[first + place]], held.at[place], sem.at[part]
            ).start()
            return carry

        lax.fori_loop(0, count, fetch, 0, unroll=4)
    copies = []
    for part, out in enumerate(outs):
        block = held.at[pl.ds(part * count, count)]
        pltpu.make_async_copy(block, block, sem.at[part]).wait()
        copies.append(pltpu.make_async_copy(block, out, sem.at[parts + part]))
        copies[-1].start()
    for copy in copies:
        copy.wait()


def gather_tiles(order, tiles, first, parts, count, name):
    block = (count,) + tiles.shape[1:]
    return pl.pallas_call(
        functools.partial(gather_kernel, first),
        out_shape=(jax.ShapeDtypeStruct(block, tiles.dtype),) * parts,
        in_specs=[SMEM, HBM],
        out_specs=(HBM,) * parts,
        scratch_shapes=[
            pltpu.VMEM((parts * count,) + tiles.shape[1:], tiles.dtype),
            pltpu.SemaphoreType.DMA((2 * parts,)),
        ],
        compiler_params=params(63),
        cost_estimate=pl.CostEstimate(
            flops=0, bytes_accessed=8 * parts * math.prod(block), transcendentals=0
        ),
        name=name,
    )(order, tiles)


def split_kernel(cut, first, second, head, tail, held, sem):
    rest = held.shape[0] - cut
    parts = (
        (first.at[pl.ds(0, cut)], held.at[pl.ds(0, cut)], head),
        (second.at[pl.ds(cut, rest)], held.at[pl.ds(cut, rest)], tail),
    )
    loads = [pltpu.make_async_copy(a, b, sem.at[i]) for i, (a, b, c) in enumerate(parts)]
    stores = [pltpu.make_async_copy(b, c, sem.at[2 + i]) for i, (a, b, c) in enumerate(parts)]
    for load in loads:
        load.start()
    for load, store in zip(loads, stores):
        load.wait()
        store.start()
    for store in stores:
        store.wait()


def split(cut, first, second):
    tile = first.shape[1:]
    return pl.pallas_call(
        functools.partial(split_kernel, cut),
        out_shape=(
            jax.ShapeDtypeStruct((cut,) + tile, first.dtype),
            jax.ShapeDtypeStruct((first.shape[0] - cut,) + tile, first.dtype),
        ),
        in_specs=[HBM, HBM],
        out_specs=(HBM, HBM),
        scratch_shapes=[pltpu.VMEM(first.shape, first.dtype), pltpu.SemaphoreType.DMA((4,))],
        compiler_params=params(63),
        cost_estimate=cost(0, 4),
        name="split",
    )(first, second)


def add_tiles(meta_ref, place, count, tiles, start, band, acc, bits):
    mask = (1 << bits) - 1
    for turn in range(count):
        meta = meta_ref[place + turn]
        row = lax.shift_right_logical(meta, bits)
        acc[row] += jnp.dot(
            tiles[start + turn], band[meta & mask], preferred_element_type=jnp.float32
        )


def sums_kernel(bits, whole, meta_keep, meta_recv, bounds, keep, recv, *rest):
    count = keep.shape[0]
    pieces, (out, band, mine, theirs, acc, sem) = rest[:-6], rest[-6:]
    size = pieces[0].shape[0]
    loads = [
        pltpu.make_async_copy(part, band.at[pl.ds(place * size, size)], sem.at[0])
        for place, part in enumerate(pieces)
    ]
    loads.append(pltpu.make_async_copy(keep, mine, sem.at[1]))
    loads.append(pltpu.make_async_copy(recv, theirs, sem.at[2]))
    for load in loads:
        load.start()
    acc[...] = jnp.zeros_like(acc)
    pltpu.make_async_copy(band, band, sem.at[0]).wait()
    for side, (meta, held) in enumerate(((meta_keep, mine), (meta_recv, theirs))):
        loads[len(pieces) + side].wait()
        if whole:

            def add(turn, carry):
                add_tiles(meta, turn * CHUNK, CHUNK, held, turn * CHUNK, band, acc, bits)
                return carry

            lax.fori_loop(0, count // CHUNK, add, 0)
        else:

            def add_one(turn, carry):
                add_tiles(meta, turn, 1, held, turn, band, acc, bits)
                return carry

            end = bounds[side]
            even = end // 8 * 8

            def add_eight(turn, carry):
                add_tiles(meta, turn * 8, 8, held, turn * 8, band, acc, bits)
                return carry

            lax.fori_loop(0, end // 8, add_eight, 0)
            lax.fori_loop(even, end, add_one, 0)
    out[...] = acc[...].astype(out.dtype)


def sums(bits, whole, dtype, meta_keep, meta_recv, bounds, keep, recv, pieces, name):
    block = pieces[0].shape
    held = pltpu.VMEM(keep.shape, keep.dtype)
    return pl.pallas_call(
        functools.partial(sums_kernel, bits, whole),
        out_shape=jax.ShapeDtypeStruct(block, dtype),
        in_specs=[SMEM] * 3 + [HBM] * (2 + len(pieces)),
        out_specs=VMEM,
        scratch_shapes=[
            pltpu.VMEM((len(pieces) * block[0],) + block[1:], jnp.bfloat16),
            held,
            held,
            pltpu.VMEM(block, jnp.float32),
            pltpu.SemaphoreType.DMA((3,)),
        ],
        compiler_params=params(63),
        cost_estimate=cost(4 * keep.size * block[2], 24),
        name=name,
    )(meta_keep, meta_recv, bounds, keep, recv, *pieces)


def final_kernel(
    bits, meta_keep, meta_recv, bounds, places, early, other, keep, recv, inbox, *rest
):
    pieces, (near, out, acc, sent, band, mine, theirs, inverse, held_near, held_out, sem, done) = (
        rest[:-12],
        rest[-12:],
    )
    count = keep.shape[0]
    size = acc.shape[0]
    loads = [pltpu.make_async_copy(early, acc, sem.at[0])]
    place = 0
    for order, piece in enumerate(pieces):
        part = band.at[pl.ds(place, piece.shape[0])]
        loads.append(pltpu.make_async_copy(piece, part, sem.at[4 + order]))
        place += piece.shape[0]
    for load in loads:
        load.start()
    others = [
        pltpu.make_async_copy(other, sent, sem.at[1]),
        pltpu.make_async_copy(inbox, inverse, sem.at[4 + len(pieces)]),
    ]
    sides = ((meta_keep, keep, mine), (meta_recv, recv, theirs))

    def chunk_copy(side, chunk):
        start = pl.multiple_of(chunk * CHUNK, CHUNK)
        piece = pl.ds(start, CHUNK)
        return pltpu.make_async_copy(
            sides[side][1].at[piece], sides[side][2].at[piece], sem.at[2 + side]
        )

    for side in (0, 1):

        def fetch(chunk, carry):
            chunk_copy(side, chunk).start()
            return carry

        lax.fori_loop(bounds[side] // CHUNK, count // CHUNK, fetch, 0)
    for load in others:
        load.start()
    for load in loads:
        load.wait()
    for side, (meta_ref, keep_ref, held) in enumerate(sides):

        def settle(chunk, carry):
            chunk_copy(side, chunk).wait()
            return carry

        lax.fori_loop(bounds[side] // CHUNK, count // CHUNK, settle, 0)

        def add(turn, carry):
            meta = meta_ref[turn]
            row = lax.shift_right_logical(meta, bits)
            slot = (meta & ((1 << bits) - 1)) - 4 * size
            acc[row] += jnp.dot(held[turn], band[slot], preferred_element_type=jnp.float32)
            return carry

        def add_eight(turn, carry):
            for step in range(8):
                add(turn * 8 + step, carry)
            return carry

        first = bounds[side]
        even = (first + 7) // 8
        lax.fori_loop(first, even * 8, add, 0)
        lax.fori_loop(even, count // 8, add_eight, 0)
    for load in others:
        load.wait()

    def apply(turn, carry):
        block = (acc[turn] + sent[turn].astype(jnp.float32)).astype(jnp.bfloat16)
        held_near[turn] = block
        held_out[turn] = jnp.dot(
            inverse[places[turn]], block, preferred_element_type=jnp.float32
        ).astype(jnp.bfloat16)
        return carry

    stores = []
    share = math.gcd(size, CHUNK)
    for order, start in enumerate(range(0, size, share)):
        lax.fori_loop(start, start + share, apply, 0, unroll=True)
        part = pl.ds(start, share)
        for side, (held, whole) in enumerate(((held_near, near), (held_out, out))):
            stores.append(
                pltpu.make_async_copy(held.at[part], whole.at[part], done.at[2 * order + side])
            )
            stores[-1].start()
    for store in stores:
        store.wait()


def final(
    bits, meta_keep, meta_recv, bounds, places, early, other, keep, recv, inbox, pieces
):
    block = early.shape
    held = pltpu.VMEM(keep.shape, keep.dtype)
    return pl.pallas_call(
        functools.partial(final_kernel, bits),
        out_shape=(jax.ShapeDtypeStruct(block, jnp.bfloat16),) * 2,
        in_specs=[SMEM] * 4 + [HBM] * (5 + len(pieces)),
        out_specs=(HBM, HBM),
        scratch_shapes=[
            pltpu.VMEM(block, jnp.float32),
            pltpu.VMEM(block, jnp.bfloat16),
            pltpu.VMEM((2 * block[0],) + block[1:], jnp.bfloat16),
            held,
            held,
            pltpu.VMEM(inbox.shape, jnp.bfloat16),
            pltpu.VMEM(block, jnp.bfloat16),
            pltpu.VMEM(block, jnp.bfloat16),
            pltpu.SemaphoreType.DMA((5 + len(pieces),)),
            pltpu.SemaphoreType.DMA((2 * block[0] // math.gcd(block[0], CHUNK),)),
        ],
        compiler_params=params(63),
        cost_estimate=cost(3 * keep.size * block[2], 22),
        name="final",
    )(meta_keep, meta_recv, bounds, places, early, other, keep, recv, inbox, *pieces)


def ranks_by(labels, key):
    same = labels[:, None] == labels[None, :]
    return jnp.sum((same & (key[:, None] > key[None, :])).astype(jnp.int32), axis=1)


def pick(values, wanted):
    position = jnp.arange(values.shape[0], dtype=jnp.int32)
    hit = wanted[:, None] == values[None, :]
    return jnp.sum(jnp.where(hit, position[None, :], 0), axis=1)


def per_device(rows, cols, sources, tiles, block_list, inverses, slot_cluster):
    size = tiles.shape[1]
    columns = sources.shape[1]
    own = sources.shape[0] // size
    devices = rows * cols
    half = cols // 2
    row = lax.axis_index("rows")
    col = lax.axis_index("cols")
    chip, core = col // 2, col % 2
    myself = row * cols + col
    blocks = sources.reshape(own, size, columns)

    def number(r, x, c):
        return r * cols + x * 2 + c

    def permute(value, pairs):
        return lax.ppermute(value, AXES, pairs)

    lines = [(x, c) for x in range(half) for c in range(2)]
    across = [
        (number(r, x, c), number(r, 1 - x, c)) for r in range(rows) for x, c in lines
    ]
    beside = [
        (number(r, x, c), number(r, x, 1 - c)) for r in range(rows) for x, c in lines
    ]
    up = [(r, r + 1) for r in range(rows - 1)]
    down = [(b, a) for a, b in up]
    early = [
        (number(a, x, c), number(b, x, c))
        for x, c in lines
        for a, b in (down if x == 0 else up)
    ]
    late = [
        (number(a, x, c), number(b, x, c))
        for x, c in lines
        for a, b in (up if x == 0 else down)
    ]

    other_chip = permute(blocks, across)
    halo_early = permute(blocks, early)
    own_beside = permute(blocks, beside)

    capacity = -(-own // devices)
    local = jnp.arange(own, dtype=jnp.int32)
    source = pick(slot_cluster, myself * own + local) // own
    places = source * capacity + ranks_by(source, local)
    held = lax.dynamic_slice_in_dim(slot_cluster, myself * own, own, 0)
    target = held // own
    place_held = target * capacity + ranks_by(target, held % own)
    outbox_order = pick(place_held, jnp.arange(devices * capacity, dtype=jnp.int32))
    (outbox,) = gather_tiles(outbox_order, inverses, 0, 1, devices * capacity, "pack_inverses")

    def exchange(value):
        return lax.all_to_all(value, AXES, split_axis=0, concat_axis=0, tiled=True)


    group = own * cols
    base = row * group
    bits = (8 * own - 1).bit_length()
    row_in = block_list[:, 0] - base
    owner = row_in // own
    column = block_list[:, 1] - base + group // 2
    quarter = column // own
    side = jnp.where(chip == 0, quarter // 2, 3 - quarter // 2)
    kind = (side + 3) % 4
    stays = owner % 2 == core
    reader = jnp.where(stays, core, 1 - core)
    slot = (jnp.minimum(kind, 2) * 2 + (quarter % 2 != reader)) * own + column % own
    meta = (row_in % own) * (1 << bits) + slot
    bucket = jnp.where(owner // 2 != chip, 0, jnp.where(kind == 3, 2, 1)) + jnp.where(stays, 0, 3)
    total = tiles.shape[0]
    quarter_count = total // 4
    index = jnp.arange(total, dtype=jnp.int32)
    key = bucket * total + index
    rank = jnp.sum((key[:, None] > key[None, :]).astype(jnp.int32), axis=1)
    placed = rank[None, :] == index[:, None]
    order = jnp.sum(jnp.where(placed, index[None, :], 0), axis=1)
    meta = jnp.sum(jnp.where(placed, meta[None, :], 0), axis=1)
    bound_keep = jnp.sum((bucket == 1).astype(jnp.int32), keepdims=True)
    bound_send = jnp.sum((bucket == 4).astype(jnp.int32), keepdims=True)
    padding = jnp.zeros((127,), jnp.int32)
    order, outbox = lax.optimization_barrier((order, outbox))
    send_cross, send_own = gather_tiles(
        order, tiles, 2 * quarter_count, 2, quarter_count, "pack_send"
    )
    recv_cross = permute(send_cross, beside)
    recv_own = permute(send_own, beside)
    meta_recv = permute(
        jnp.concatenate([meta[2 * quarter_count :], bound_send, padding]), beside
    )
    keep_cross, keep_own = gather_tiles(
        order, tiles, 0, 2, quarter_count, "pack_keep"
    )
    bounds = jnp.concatenate([bound_keep, meta_recv[2 * quarter_count : 2 * quarter_count + 1]])

    own_keep = meta[quarter_count : 2 * quarter_count]
    own_recv = meta_recv[quarter_count : 2 * quarter_count]
    cross_keep = meta[:quarter_count]
    cross_recv = meta_recv[:quarter_count]
    (
        other_chip,
        halo_early,
        keep_cross,
        keep_own,
        outbox,
        bounds,
        own_keep,
        own_recv,
        cross_keep,
        cross_recv,
        places,
    ) = lax.optimization_barrier(
        (
            other_chip,
            halo_early,
            keep_cross,
            keep_own,
            outbox,
            bounds,
            own_keep,
            own_recv,
            cross_keep,
            cross_recv,
            places,
        )
    )

    other_beside = permute(other_chip, beside)
    cut = own - own // 4
    late_part, across_part = split(cut, other_chip, halo_early)
    halo_late = permute(late_part, late)
    halo_across = permute(across_part, across)
    inbox = exchange(outbox)
    early_beside = permute(halo_early, beside)
    group_pieces = (blocks, own_beside, other_chip, other_beside)
    cross = sums(
        bits,
        True,
        jnp.bfloat16,
        cross_keep,
        cross_recv,
        bounds,
        keep_cross,
        recv_cross,
        group_pieces + (halo_early, early_beside),
        "cross",
    )
    other_sums = permute(cross, across)
    own_keep, halo_across = lax.optimization_barrier((own_keep, halo_across))
    early_sums = sums(
        bits,
        False,
        jnp.float32,
        own_keep,
        own_recv,
        bounds,
        keep_own,
        recv_own,
        group_pieces,
        "own",
    )
    halo_late, early_sums = lax.optimization_barrier((halo_late, early_sums))
    late_beside = permute(halo_late, beside)
    across_beside = permute(halo_across, beside)
    near, result = final(
        bits,
        own_keep,
        own_recv,
        bounds,
        places,
        early_sums,
        other_sums,
        keep_own,
        recv_own,
        inbox,
        (halo_late, halo_across, late_beside, across_beside),
    )
    return near.reshape(own * size, columns), result.reshape(own * size, columns)


def solution(mesh):
    spec = P(AXES, None)
    spec3 = P(AXES, None, None)
    return jax.shard_map(
        functools.partial(per_device, mesh.shape["rows"], mesh.shape["cols"]),
        mesh=mesh,
        in_specs=(spec, spec3, spec, spec3, P()),
        out_specs=(spec, spec),
        check_vma=False,
    )
```

```python
import functools
import math

import jax
import jax.numpy as jnp
from jax import lax
from jax.experimental import pallas as pl
from jax.experimental.pallas import tpu as pltpu
from jax.sharding import PartitionSpec as P

AXES = ("rows", "cols")
MIB = 1024 * 1024
HBM = pl.BlockSpec(memory_space=pltpu.HBM)
SMEM = pl.BlockSpec(memory_space=pltpu.SMEM)
VMEM = pl.BlockSpec(memory_space=pltpu.VMEM)
CHUNK = 16


def params(mib):
    return pltpu.CompilerParams(vmem_limit_bytes=mib * MIB)


def cost(flops, mib):
    return pl.CostEstimate(flops=flops, bytes_accessed=mib * MIB, transcendentals=0)


def gather_kernel(first, order_ref, tiles, *rest):
    outs, (held, sem) = rest[:-2], rest[-2:]
    parts = len(outs)
    count = outs[0].shape[0]
    for part in range(parts):

        def fetch(turn, carry):
            place = part * count + turn
            pltpu.make_async_copy(
                tiles.at[order_ref[first + place]], held.at[place], sem.at[part]
            ).start()
            return carry

        lax.fori_loop(0, count, fetch, 0, unroll=4)
    copies = []
    for part, out in enumerate(outs):
        block = held.at[pl.ds(part * count, count)]
        pltpu.make_async_copy(block, block, sem.at[part]).wait()
        copies.append(pltpu.make_async_copy(block, out, sem.at[parts + part]))
        copies[-1].start()
    for copy in copies:
        copy.wait()


def gather_tiles(order, tiles, first, parts, count, name):
    block = (count,) + tiles.shape[1:]
    return pl.pallas_call(
        functools.partial(gather_kernel, first),
        out_shape=(jax.ShapeDtypeStruct(block, tiles.dtype),) * parts,
        in_specs=[SMEM, HBM],
        out_specs=(HBM,) * parts,
        scratch_shapes=[
            pltpu.VMEM((parts * count,) + tiles.shape[1:], tiles.dtype),
            pltpu.SemaphoreType.DMA((2 * parts,)),
        ],
        compiler_params=params(63),
        cost_estimate=pl.CostEstimate(
            flops=0, bytes_accessed=8 * parts * math.prod(block), transcendentals=0
        ),
        name=name,
    )(order, tiles)


def split_kernel(cut, first, second, head, tail, held, sem):
    rest = held.shape[0] - cut
    parts = (
        (first.at[pl.ds(0, cut)], held.at[pl.ds(0, cut)], head),
        (second.at[pl.ds(cut, rest)], held.at[pl.ds(cut, rest)], tail),
    )
    loads = [pltpu.make_async_copy(a, b, sem.at[i]) for i, (a, b, c) in enumerate(parts)]
    stores = [pltpu.make_async_copy(b, c, sem.at[2 + i]) for i, (a, b, c) in enumerate(parts)]
    for load in loads:
        load.start()
    for load, store in zip(loads, stores):
        load.wait()
        store.start()
    for store in stores:
        store.wait()


def split(cut, first, second):
    tile = first.shape[1:]
    return pl.pallas_call(
        functools.partial(split_kernel, cut),
        out_shape=(
            jax.ShapeDtypeStruct((cut,) + tile, first.dtype),
            jax.ShapeDtypeStruct((first.shape[0] - cut,) + tile, first.dtype),
        ),
        in_specs=[HBM, HBM],
        out_specs=(HBM, HBM),
        scratch_shapes=[pltpu.VMEM(first.shape, first.dtype), pltpu.SemaphoreType.DMA((4,))],
        compiler_params=params(63),
        cost_estimate=cost(0, 4),
        name="split",
    )(first, second)


def add_tiles(meta_ref, place, count, tiles, start, band, acc, bits):
    mask = (1 << bits) - 1
    for turn in range(count):
        meta = meta_ref[place + turn]
        row = lax.shift_right_logical(meta, bits)
        acc[row] += jnp.dot(
            tiles[start + turn], band[meta & mask], preferred_element_type=jnp.float32
        )


def sums_kernel(bits, whole, meta_keep, meta_recv, bounds, keep, recv, *rest):
    count = keep.shape[0]
    pieces, (out, band, mine, theirs, acc, sem) = rest[:-6], rest[-6:]
    size = pieces[0].shape[0]
    loads = [
        pltpu.make_async_copy(part, band.at[pl.ds(place * size, size)], sem.at[0])
        for place, part in enumerate(pieces)
    ]
    loads.append(pltpu.make_async_copy(keep, mine, sem.at[1]))
    loads.append(pltpu.make_async_copy(recv, theirs, sem.at[2]))
    for load in loads:
        load.start()
    acc[...] = jnp.zeros_like(acc)
    pltpu.make_async_copy(band, band, sem.at[0]).wait()
    for side, (meta, held) in enumerate(((meta_keep, mine), (meta_recv, theirs))):
        loads[len(pieces) + side].wait()
        if whole:

            def add(turn, carry):
                add_tiles(meta, turn * CHUNK, CHUNK, held, turn * CHUNK, band, acc, bits)
                return carry

            lax.fori_loop(0, count // CHUNK, add, 0)
        else:

            def add_one(turn, carry):
                add_tiles(meta, turn, 1, held, turn, band, acc, bits)
                return carry

            end = bounds[side]
            even = end // 8 * 8

            def add_eight(turn, carry):
                add_tiles(meta, turn * 8, 8, held, turn * 8, band, acc, bits)
                return carry

            lax.fori_loop(0, end // 8, add_eight, 0)
            lax.fori_loop(even, end, add_one, 0)
    out[...] = acc[...].astype(out.dtype)


def sums(bits, whole, dtype, meta_keep, meta_recv, bounds, keep, recv, pieces, name):
    block = pieces[0].shape
    held = pltpu.VMEM(keep.shape, keep.dtype)
    return pl.pallas_call(
        functools.partial(sums_kernel, bits, whole),
        out_shape=jax.ShapeDtypeStruct(block, dtype),
        in_specs=[SMEM] * 3 + [HBM] * (2 + len(pieces)),
        out_specs=VMEM,
        scratch_shapes=[
            pltpu.VMEM((len(pieces) * block[0],) + block[1:], jnp.bfloat16),
            held,
            held,
            pltpu.VMEM(block, jnp.float32),
            pltpu.SemaphoreType.DMA((3,)),
        ],
        compiler_params=params(63),
        cost_estimate=cost(4 * keep.size * block[2], 24),
        name=name,
    )(meta_keep, meta_recv, bounds, keep, recv, *pieces)


def final_kernel(
    bits, meta_keep, meta_recv, bounds, places, early, other, keep, recv, inbox, *rest
):
    pieces, (near, out, acc, sent, band, mine, theirs, inverse, held_near, held_out, sem, done) = (
        rest[:-12],
        rest[-12:],
    )
    count = keep.shape[0]
    size = acc.shape[0]
    loads = [pltpu.make_async_copy(early, acc, sem.at[0])]
    place = 0
    for order, piece in enumerate(pieces):
        part = band.at[pl.ds(place, piece.shape[0])]
        loads.append(pltpu.make_async_copy(piece, part, sem.at[4 + order]))
        place += piece.shape[0]
    for load in loads:
        load.start()
    others = [
        pltpu.make_async_copy(other, sent, sem.at[1]),
        pltpu.make_async_copy(inbox, inverse, sem.at[4 + len(pieces)]),
    ]
    sides = ((meta_keep, keep, mine), (meta_recv, recv, theirs))

    def chunk_copy(side, chunk):
        start = pl.multiple_of(chunk * CHUNK, CHUNK)
        piece = pl.ds(start, CHUNK)
        return pltpu.make_async_copy(
            sides[side][1].at[piece], sides[side][2].at[piece], sem.at[2 + side]
        )

    for side in (0, 1):

        def fetch(chunk, carry):
            chunk_copy(side, chunk).start()
            return carry

        lax.fori_loop(bounds[side] // CHUNK, count // CHUNK, fetch, 0)
    for load in others:
        load.start()
    for load in loads:
        load.wait()
    for side, (meta_ref, keep_ref, held) in enumerate(sides):

        def settle(chunk, carry):
            chunk_copy(side, chunk).wait()
            return carry

        lax.fori_loop(bounds[side] // CHUNK, count // CHUNK, settle, 0)

        def add(turn, carry):
            meta = meta_ref[turn]
            row = lax.shift_right_logical(meta, bits)
            slot = (meta & ((1 << bits) - 1)) - 4 * size
            acc[row] += jnp.dot(held[turn], band[slot], preferred_element_type=jnp.float32)
            return carry

        def add_eight(turn, carry):
            for step in range(8):
                add(turn * 8 + step, carry)
            return carry

        first = bounds[side]
        even = (first + 7) // 8
        lax.fori_loop(first, even * 8, add, 0)
        lax.fori_loop(even, count // 8, add_eight, 0)
    for load in others:
        load.wait()

    def apply(turn, carry):
        block = (acc[turn] + sent[turn].astype(jnp.float32)).astype(jnp.bfloat16)
        held_near[turn] = block
        held_out[turn] = jnp.dot(
            inverse[places[turn]], block, preferred_element_type=jnp.float32
        ).astype(jnp.bfloat16)
        return carry

    stores = []
    share = math.gcd(size, CHUNK)
    for order, start in enumerate(range(0, size, share)):
        lax.fori_loop(start, start + share, apply, 0, unroll=True)
        part = pl.ds(start, share)
        for side, (held, whole) in enumerate(((held_near, near), (held_out, out))):
            stores.append(
                pltpu.make_async_copy(held.at[part], whole.at[part], done.at[2 * order + side])
            )
            stores[-1].start()
    for store in stores:
        store.wait()


def final(
    bits, meta_keep, meta_recv, bounds, places, early, other, keep, recv, inbox, pieces
):
    block = early.shape
    held = pltpu.VMEM(keep.shape, keep.dtype)
    return pl.pallas_call(
        functools.partial(final_kernel, bits),
        out_shape=(jax.ShapeDtypeStruct(block, jnp.bfloat16),) * 2,
        in_specs=[SMEM] * 4 + [HBM] * (5 + len(pieces)),
        out_specs=(HBM, HBM),
        scratch_shapes=[
            pltpu.VMEM(block, jnp.float32),
            pltpu.VMEM(block, jnp.bfloat16),
            pltpu.VMEM((2 * block[0],) + block[1:], jnp.bfloat16),
            held,
            held,
            pltpu.VMEM(inbox.shape, jnp.bfloat16),
            pltpu.VMEM(block, jnp.bfloat16),
            pltpu.VMEM(block, jnp.bfloat16),
            pltpu.SemaphoreType.DMA((5 + len(pieces),)),
            pltpu.SemaphoreType.DMA((2 * block[0] // math.gcd(block[0], CHUNK),)),
        ],
        compiler_params=params(63),
        cost_estimate=cost(3 * keep.size * block[2], 22),
        name="final",
    )(meta_keep, meta_recv, bounds, places, early, other, keep, recv, inbox, *pieces)


def ranks_by(labels, key):
    same = labels[:, None] == labels[None, :]
    return jnp.sum((same & (key[:, None] > key[None, :])).astype(jnp.int32), axis=1)


def pick(values, wanted):
    position = jnp.arange(values.shape[0], dtype=jnp.int32)
    hit = wanted[:, None] == values[None, :]
    return jnp.sum(jnp.where(hit, position[None, :], 0), axis=1)


def per_device(rows, cols, sources, tiles, block_list, inverses, slot_cluster):
    size = tiles.shape[1]
    columns = sources.shape[1]
    own = sources.shape[0] // size
    devices = rows * cols
    half = cols // 2
    row = lax.axis_index("rows")
    col = lax.axis_index("cols")
    chip, core = col // 2, col % 2
    myself = row * cols + col
    blocks = sources.reshape(own, size, columns)

    def number(r, x, c):
        return r * cols + x * 2 + c

    def permute(value, pairs):
        return lax.ppermute(value, AXES, pairs)

    lines = [(x, c) for x in range(half) for c in range(2)]
    across = [
        (number(r, x, c), number(r, 1 - x, c)) for r in range(rows) for x, c in lines
    ]
    beside = [
        (number(r, x, c), number(r, x, 1 - c)) for r in range(rows) for x, c in lines
    ]
    up = [(r, r + 1) for r in range(rows - 1)]
    down = [(b, a) for a, b in up]
    early = [
        (number(a, x, c), number(b, x, c))
        for x, c in lines
        for a, b in (down if x == 0 else up)
    ]
    late = [
        (number(a, x, c), number(b, x, c))
        for x, c in lines
        for a, b in (up if x == 0 else down)
    ]

    other_chip = permute(blocks, across)
    halo_early = permute(blocks, early)
    own_beside = permute(blocks, beside)

    capacity = -(-own // devices)
    local = jnp.arange(own, dtype=jnp.int32)
    source = pick(slot_cluster, myself * own + local) // own
    places = source * capacity + ranks_by(source, local)
    held = lax.dynamic_slice_in_dim(slot_cluster, myself * own, own, 0)
    target = held // own
    place_held = target * capacity + ranks_by(target, held % own)
    outbox_order = pick(place_held, jnp.arange(devices * capacity, dtype=jnp.int32))
    (outbox,) = gather_tiles(outbox_order, inverses, 0, 1, devices * capacity, "pack_inverses")

    def exchange(value):
        return lax.all_to_all(value, AXES, split_axis=0, concat_axis=0, tiled=True)


    group = own * cols
    base = row * group
    bits = (8 * own - 1).bit_length()
    row_in = block_list[:, 0] - base
    owner = row_in // own
    column = block_list[:, 1] - base + group // 2
    quarter = column // own
    side = jnp.where(chip == 0, quarter // 2, 3 - quarter // 2)
    kind = (side + 3) % 4
    stays = owner % 2 == core
    reader = jnp.where(stays, core, 1 - core)
    slot = (jnp.minimum(kind, 2) * 2 + (quarter % 2 != reader)) * own + column % own
    meta = (row_in % own) * (1 << bits) + slot
    bucket = jnp.where(owner // 2 != chip, 0, jnp.where(kind == 3, 2, 1)) + jnp.where(stays, 0, 3)
    total = tiles.shape[0]
    quarter_count = total // 4
    index = jnp.arange(total, dtype=jnp.int32)
    key = bucket * total + index
    rank = jnp.sum((key[:, None] > key[None, :]).astype(jnp.int32), axis=1)
    placed = rank[None, :] == index[:, None]
    order = jnp.sum(jnp.where(placed, index[None, :], 0), axis=1)
    meta = jnp.sum(jnp.where(placed, meta[None, :], 0), axis=1)
    bound_keep = jnp.sum((bucket == 1).astype(jnp.int32), keepdims=True)
    bound_send = jnp.sum((bucket == 4).astype(jnp.int32), keepdims=True)
    padding = jnp.zeros((127,), jnp.int32)
    order, outbox = lax.optimization_barrier((order, outbox))
    send_cross, send_own = gather_tiles(
        order, tiles, 2 * quarter_count, 2, quarter_count, "pack_send"
    )
    recv_cross = permute(send_cross, beside)
    recv_own = permute(send_own, beside)
    meta_recv = permute(
        jnp.concatenate([meta[2 * quarter_count :], bound_send, padding]), beside
    )
    keep_cross, keep_own = gather_tiles(
        order, tiles, 0, 2, quarter_count, "pack_keep"
    )
    bounds = jnp.concatenate([bound_keep, meta_recv[2 * quarter_count : 2 * quarter_count + 1]])

    own_keep = meta[quarter_count : 2 * quarter_count]
    own_recv = meta_recv[quarter_count : 2 * quarter_count]
    cross_keep = meta[:quarter_count]
    cross_recv = meta_recv[:quarter_count]
    (
        other_chip,
        halo_early,
        keep_cross,
        keep_own,
        outbox,
        bounds,
        own_keep,
        own_recv,
        cross_keep,
        cross_recv,
        places,
    ) = lax.optimization_barrier(
        (
            other_chip,
            halo_early,
            keep_cross,
            keep_own,
            outbox,
            bounds,
            own_keep,
            own_recv,
            cross_keep,
            cross_recv,
            places,
        )
    )

    other_beside = permute(other_chip, beside)
    cut = own - 3 * own // 8
    late_part, across_part = split(cut, other_chip, halo_early)
    halo_late = permute(late_part, late)
    halo_across = permute(across_part, across)
    inbox = exchange(outbox)
    early_beside = permute(halo_early, beside)
    group_pieces = (blocks, own_beside, other_chip, other_beside)
    cross = sums(
        bits,
        True,
        jnp.bfloat16,
        cross_keep,
        cross_recv,
        bounds,
        keep_cross,
        recv_cross,
        group_pieces + (halo_early, early_beside),
        "cross",
    )
    other_sums = permute(cross, across)
    own_keep, halo_across = lax.optimization_barrier((own_keep, halo_across))
    early_sums = sums(
        bits,
        False,
        jnp.float32,
        own_keep,
        own_recv,
        bounds,
        keep_own,
        recv_own,
        group_pieces,
        "own",
    )
    halo_late, early_sums = lax.optimization_barrier((halo_late, early_sums))
    late_beside = permute(halo_late, beside)
    across_beside = permute(halo_across, beside)
    near, result = final(
        bits,
        own_keep,
        own_recv,
        bounds,
        places,
        early_sums,
        other_sums,
        keep_own,
        recv_own,
        inbox,
        (halo_late, halo_across, late_beside, across_beside),
    )
    return near.reshape(own * size, columns), result.reshape(own * size, columns)


def solution(mesh):
    spec = P(AXES, None)
    spec3 = P(AXES, None, None)
    return jax.shard_map(
        functools.partial(per_device, mesh.shape["rows"], mesh.shape["cols"]),
        mesh=mesh,
        in_specs=(spec, spec3, spec, spec3, P()),
        out_specs=(spec, spec),
        check_vma=False,
    )
```
